32 devices in a mesh: gx: 4 (over z), gy: 4 (over y, core), gz: 2 (over x).
Axes of the slice: x: 2, y: 2, z: 4, core: 2. Of those that a mesh axis runs over, the one named last changes fastest.
Arguments:
- solution: float32 [3, 32, 64, 256], P(None, 'gx', 'gy', 'gz'), may hold values from -6 to 6
- residual: float32 [3, 32, 64, 256], P(None, 'gx', 'gy', 'gz'), may hold values from -15 to 15
- density_bins: int32 [32, 64, 256], P('gx', 'gy', 'gz'), may hold values from 0 to 15
- fixed_dofs: int32 [3, 32, 64, 256], P(None, 'gx', 'gy', 'gz'), may hold values from 0 to 1
Outputs:
- solution_next: float32 [3, 32, 64, 256], P(None, 'gx', 'gy', 'gz')
- residual_next: float32 [3, 32, 64, 256], P(None, 'gx', 'gy', 'gz')
- direction: float32 [3, 32, 64, 256], P(None, 'gx', 'gy', 'gz')
The draws below stay inside these ranges and needn't reach their ends.
All inputs are finite; a program needn't handle non-finite values.
Results may differ from the reference program's by a relative error of at most 0.0003.
Values sent between devices are 32-bit elements; how exact they have to be, the bound alone decides.
A program may use at most 64 MiB of HBM per device.

```python
import jax
import jax.numpy as jnp

CX = 8
COMP = 3
SWEEPS = 3
BINS = 16
NX = 32
NY = 64
NZ = 256


def draw_residual(key, part):
    key = jax.random.fold_in(key, 11)
    along_x = jnp.arange(NX, dtype=jnp.float32) / (NX - 1)
    along_y = jnp.arange(NY, dtype=jnp.float32) / (NY - 1)
    along_z = jnp.arange(NZ, dtype=jnp.float32) / (NZ - 1)
    smooth = (along_z * along_z)[None, None, :] + 0.0 * along_y[None, :, None]
    base = jnp.clip(jax.random.normal(key, (COMP, NX, NY, NZ), jnp.float32), -4.0, 4.0)
    scale = (1.0 + 2.0 * along_x)[:, None, None] + 0.0 * along_y[None, :, None]
    return (base * scale[None] + smooth[None]).astype(jnp.float32)


def draw_density_bins(key, part):
    key = jax.random.fold_in(key, 23)
    key_flip, key_soft, key_hard = jax.random.split(key, 3)
    flip = jax.random.randint(key_flip, (), 0, 2)
    layer = (jnp.arange(NX, dtype=jnp.int32) // CX + flip) % 2
    softer = jax.random.randint(key_soft, (NX, NY, NZ), 0, 6)
    harder = jax.random.randint(key_hard, (NX, NY, NZ), 10, 16)
    return jnp.where(layer[:, None, None] == 0, softer, harder).astype(jnp.int32)


def draw_fixed_dofs(key, part):
    key = jax.random.fold_in(key, 37)
    level = 1 + 7 * jnp.arange(NZ, dtype=jnp.int32) // (NZ - 1)
    picks = jax.random.randint(key, (COMP, NX, NY, NZ), 0, 16)
    return (picks < level[None, None, None, :]).astype(jnp.int32)


def block_scale(stream_key, extent, pieces, low, high):
    gain, own = 1.0, jax.random.fold_in(stream_key, 6)
    for axis_at, parts in pieces:
        heights = jnp.exp(jax.random.uniform(jax.random.fold_in(own, axis_at), (parts,), jnp.float32, low / len(pieces), high / len(pieces)))
        gain = gain * jnp.repeat(heights, extent[axis_at] // parts).reshape([-1 if axis == axis_at else 1 for axis in range(len(extent))])
    return gain


def centred(key, dims, width, bound, cuts=(), held_as=jnp.bfloat16):
    entries = jax.random.normal(key, dims, jnp.float32) * width
    if len(cuts) > 0:
        entries = block_scale(key, dims, cuts, -0.22, 0.18) * entries
    return jnp.clip(entries, min=-bound, max=bound).astype(held_as)


def setup_inputs(seed: int = 0) -> dict:
    keys = jax.random.split(jax.random.key(seed), 5)
    solution = centred(keys[0], (COMP, NX, NY, NZ), 1.0, 6.0, ((1, 4), (2, 4), (3, 2)), jnp.float32)
    residual = draw_residual(jax.random.fold_in(keys[4], 71), 0)
    density_bins = draw_density_bins(jax.random.fold_in(keys[4], 71), 0)
    fixed_dofs = draw_fixed_dofs(jax.random.fold_in(keys[4], 71), 0)
    return dict(solution=solution, residual=residual, density_bins=density_bins, fixed_dofs=fixed_dofs)


damping = 0.6
eig_center = 1.05
eig_halfwidth = 0.95


def stiffness(density_bins):
    fraction = (density_bins.astype(jnp.float32) + 1.0) / BINS
    return 0.05 + 0.95 * fraction * fraction * fraction


def couplings(padded):
    center = padded[1:-1, 1:-1, 1:-1]

    def shared(other):
        return jnp.where(other > 0.0, 0.5 * (center + other), 0.0)

    upper = jnp.stack([shared(padded[2:, 1:-1, 1:-1]), shared(padded[1:-1, 2:, 1:-1]), shared(padded[1:-1, 1:-1, 2:])])
    lower = jnp.stack([shared(padded[:-2, 1:-1, 1:-1]), shared(padded[1:-1, :-2, 1:-1]), shared(padded[1:-1, 1:-1, :-2])])
    return upper, lower


def level_apply(field, padded, upper, lower, spring):
    total = spring * field
    total = total + upper[0] * (field - padded[:, 2:, 1:-1, 1:-1]) + lower[0] * (field - padded[:, :-2, 1:-1, 1:-1])
    total = total + upper[1] * (field - padded[:, 1:-1, 2:, 1:-1]) + lower[1] * (field - padded[:, 1:-1, :-2, 1:-1])
    total = total + upper[2] * (field - padded[:, 1:-1, 1:-1, 2:]) + lower[2] * (field - padded[:, 1:-1, 1:-1, :-2])
    return total


def level_diagonal(upper, lower, spring):
    return jnp.sum(upper, axis=0) + jnp.sum(lower, axis=0) + spring


def restrict(field):
    channels, size_x, size_y, size_z = field.shape
    return field.reshape(channels, size_x // 2, 2, size_y // 2, 2, size_z // 2, 2).sum(axis=(2, 4, 6))


def prolong(field):
    return jnp.repeat(jnp.repeat(jnp.repeat(field, 2, axis=1), 2, axis=2), 2, axis=3)


def coarse_links(links, offset):
    size_x, size_y, size_z = links.shape[1:]
    along_x = links[0][offset::2].reshape(size_x // 2, size_y // 2, 2, size_z // 2, 2).sum(axis=(2, 4))
    along_y = links[1][:, offset::2].reshape(size_x // 2, 2, size_y // 2, size_z // 2, 2).sum(axis=(1, 4))
    along_z = links[2][:, :, offset::2].reshape(size_x // 2, 2, size_y // 2, 2, size_z // 2).sum(axis=(1, 3))
    return jnp.stack([along_x, along_y, along_z])


def zero_rim(field):
    return jnp.pad(field, ((0, 0), (1, 1), (1, 1), (1, 1)))


def chebyshev(rhs, upper, lower, spring, diagonal, with_rim):
    ratio = eig_center / eig_halfwidth
    factor = 1.0 / ratio
    update = rhs / (eig_center * diagonal)
    iterate = update
    for step_index in range(SWEEPS - 1):
        remainder = rhs - level_apply(iterate, with_rim(iterate), upper, lower, spring)
        next_factor = 1.0 / (2.0 * ratio - factor)
        update = next_factor * factor * update + (2.0 * next_factor / eig_halfwidth) * remainder / diagonal
        iterate = iterate + update
        factor = next_factor
    return iterate


def reference(solution, residual, density_bins, fixed_dofs):
    fixed = fixed_dofs.astype(jnp.float32)
    free = 1.0 - fixed
    modulus = stiffness(density_bins)
    fine_upper, fine_lower = couplings(jnp.pad(modulus, 1))
    fine_spring = 0.1 * modulus
    fine_diag = free * level_diagonal(fine_upper, fine_lower, fine_spring) + fixed

    def fine_apply(field):
        masked = free * field
        return free * level_apply(masked, zero_rim(masked), fine_upper, fine_lower, fine_spring) + fixed * field

    mid_upper = coarse_links(fine_upper, 1)
    mid_lower = coarse_links(fine_lower, 0)
    mid_spring = restrict(fine_spring[None])[0]
    mid_diag = level_diagonal(mid_upper, mid_lower, mid_spring)
    low_upper = coarse_links(mid_upper, 1)
    low_lower = coarse_links(mid_lower, 0)
    low_spring = restrict(mid_spring[None])[0]
    low_diag = level_diagonal(low_upper, low_lower, low_spring)

    fine_corr = damping * residual / fine_diag
    mid_rhs = restrict(residual - fine_apply(fine_corr))
    mid_corr = damping * mid_rhs / mid_diag
    coarse_rhs = restrict(mid_rhs - level_apply(mid_corr, zero_rim(mid_corr), mid_upper, mid_lower, mid_spring))
    coarse_corr = chebyshev(coarse_rhs, low_upper, low_lower, low_spring, low_diag, zero_rim)
    mid_corr = mid_corr + prolong(coarse_corr)
    mid_corr = mid_corr + damping * (mid_rhs - level_apply(mid_corr, zero_rim(mid_corr), mid_upper, mid_lower, mid_spring)) / mid_diag
    fine_corr = fine_corr + prolong(mid_corr)
    direction = fine_corr + damping * (residual - fine_apply(fine_corr)) / fine_diag
    image = fine_apply(direction)
    alpha = jnp.sum(residual * direction) / jnp.sum(direction * image)
    return solution + alpha * direction, residual - alpha * image, direction
```

```python
import functools

import jax
import jax.numpy as jnp
from jax import lax
from jax.experimental import pallas as pl
from jax.experimental.pallas import tpu as pltpu
from jax.sharding import PartitionSpec as P

SWEEPS = 3
BINS = 16
AXES = ("gx", "gy", "gz")

damping = 0.6
eig_center = 1.05
eig_halfwidth = 0.95

ROUNDS = ("bins", 0, 1, 2, 2, 1, 0, 0)


def roll(v, shift, axis):
    shift = shift % v.shape[axis]
    return v if shift == 0 else pltpu.roll(v, shift, axis)


def iota(shape, dim):
    return lax.broadcasted_iota(jnp.int32, shape, dim)


def pair_sum(v, s, axis):
    even = (iota(v.shape, axis) // s) % 2 == 0
    return v + jnp.where(even, roll(v, -s, axis), roll(v, s, axis))


def restrict(v, s):
    lead = v.shape[:-3]
    nx, ny, nz = v.shape[-3:]
    w = v.reshape(lead + (nx // 2, 2, ny, nz))
    k = len(lead) + 1
    w = lax.index_in_dim(w, 0, k, False) + lax.index_in_dim(w, 1, k, False)
    return pair_sum(pair_sum(w, s, w.ndim - 2), s, w.ndim - 1)


def prolong(v):
    c, nx, ny, nz = v.shape
    return jnp.broadcast_to(v[:, :, None], (c, nx, 2, ny, nz)).reshape(c, 2 * nx, ny, nz)


def kernel(counts, sol, res, den, fix, out_s, out_r, out_d, *scratch):
    n_rounds = len(ROUNDS)
    bufs = [scratch[6 * r : 6 * r + 6] for r in range(n_rounds)]
    rest = scratch[6 * n_rounds :]
    coef = rest[0:3]
    free_ref, diag_ref, inv_ref, fc0_ref, inv1_ref, inv2_ref = rest[3:9]
    sums = rest[9:12]
    part, send_sem, recv_sem, ssend_sem, srecv_sem = rest[12:17]

    idx = [lax.axis_index(a) for a in AXES]
    ny, nz = den.shape[1:]
    half = ny // 2

    for r in range(n_rounds):
        _, xr, _, yr, _, zr = bufs[r]
        xr[...] = jnp.zeros_like(xr)
        yr[...] = jnp.zeros_like(yr)
        zr[...] = jnp.zeros_like(zr)

    barrier = pltpu.get_barrier_semaphore()
    for a, axis in enumerate(AXES):
        for k in range(1, counts[a]):
            pl.semaphore_signal(
                barrier,
                inc=1,
                device_id={axis: lax.rem(idx[a] + k, counts[a])},
                device_id_type=pl.DeviceIdType.MESH,
            )
    pl.semaphore_wait(barrier, sum(c - 1 for c in counts))

    def copies(r, a):
        field, xr, ys, yr, zs, zr = bufs[r]
        nx = field.shape[1]
        for up in (0, 1):
            if a == 0:
                src = field.at[:, pl.ds(0 if up else nx - 1, 1)]
                dst = xr.at[up]
            elif a == 1:
                src, dst = ys.at[up], yr.at[up]
            else:
                src, dst = zs, zr.at[up]
            slot = 2 * a + up
            yield pltpu.make_async_remote_copy(
                src_ref=src,
                dst_ref=dst,
                send_sem=send_sem.at[r, slot],
                recv_sem=recv_sem.at[r, slot],
                device_id={AXES[a]: idx[a] - 1 if up else idx[a] + 1},
                device_id_type=pl.DeviceIdType.MESH,
            )

    def has_next(a):
        return idx[a] < counts[a] - 1

    def has_prev(a):
        return idx[a] > 0

    def start(r, a):
        to_next, to_prev = copies(r, a)
        pl.when(has_next(a))(to_next.start)
        pl.when(has_prev(a))(to_prev.start)

    def wait(r, a):
        to_next, to_prev = copies(r, a)
        pl.when(has_prev(a))(to_next.wait_recv)
        pl.when(has_next(a))(to_prev.wait_recv)

    def send(r, v, s):
        field, xr, ys, yr, zs, zr = bufs[r]
        c, nx = v.shape[:2]
        field[...] = v
        start(r, 0)
        ys[0] = v[:, :, ny - 1 : ny]
        ys[1] = v[:, :, 0:1]
        start(r, 1)
        place = ((iota((ny, nz), 1) + s) % nz) // (2 * s)
        packed = jnp.zeros((ny, nz), jnp.float32)
        for p in range(c * nx):
            packed = jnp.where(place == p, roll(v[p // nx, p % nx], 2 * s * p, 1), packed)
        zs[...] = packed
        start(r, 2)

    def z_halo(r, s):
        field, _, _, _, _, zr = bufs[r]
        c, nx = field.shape[:2]
        wait(r, 2)
        even = (iota((ny, nz), 1) // s) % 2 == 0
        w = jnp.where(even, roll(zr[0], s, 1), roll(zr[1], -s, 1))
        planes = [roll(w, -2 * s * p, 1) for p in range(c * nx)]
        return jnp.stack(planes).reshape(c, nx, ny, nz)

    def set_coef(level, lows, ups):
        ref = coef[level]
        s = 2**level
        shape = lows[0].shape
        row, lane = iota(shape, 1), iota(shape, 2)
        zero = jnp.zeros(shape, jnp.float32)
        ref[0] = lows[0]
        ref[1] = ups[0]
        ref[2] = jnp.where(row >= s, lows[1], zero)
        ref[3] = jnp.where(row < ny - s, ups[1], zero)
        ref[4] = jnp.where(lane >= s, lows[2], zero)
        ref[5] = jnp.where(lane < nz - s, ups[2], zero)
        ref[6] = jnp.where(row < s, lows[1], jnp.where(row >= ny - s, ups[1], zero))
        ref[7] = jnp.where(lane < s, lows[2], jnp.where(lane >= nz - s, ups[2], zero))

    def local_sum(level, v):
        ref = coef[level]
        s = 2**level
        edge = jnp.zeros_like(v[:, :1])
        total = ref[0] * jnp.concatenate([edge, v[:, :-1]], 1)
        total = total + ref[1] * jnp.concatenate([v[:, 1:], edge], 1)
        total = total + ref[2] * roll(v, s, 2) + ref[3] * roll(v, -s, 2)
        return total + ref[4] * roll(v, s, 3) + ref[5] * roll(v, -s, 3)

    def halo_sum(level, r, total):
        ref = coef[level]
        s = 2**level
        _, xr, _, yr, _, _ = bufs[r]
        nx = total.shape[1]
        wait(r, 0)
        first = total[:, :1] + ref[0, 0:1] * xr[0]
        last = total[:, nx - 1 :] + ref[1, nx - 1 : nx] * xr[1]
        middle = [total[:, 1 : nx - 1]] if nx > 2 else []
        total = jnp.concatenate([first] + middle + [last], 1)
        wait(r, 1)
        top = total[:, :, :half] + ref[6, :, :half] * yr[0]
        bottom = total[:, :, half:] + ref[6, :, half:] * yr[1]
        total = jnp.concatenate([top, bottom], 2)
        return total + ref[7] * z_halo(r, s)

    def neighbours(level, r, v):
        send(r, v, 2**level)
        return halo_sum(level, r, local_sum(level, v))

    def coarse_links(level, lows, ups):
        s = 2**level
        nx = lows[0].shape[0]
        row = (iota(lows[0].shape, 1) // s) % 2
        lane = (iota(lows[0].shape, 2) // s) % 2

        def along_x(links, offset):
            w = links.reshape(nx // 2, 2, ny, nz)[:, offset]
            return pair_sum(pair_sum(w, s, 1), s, 2)

        low = [
            along_x(lows[0], 0),
            restrict(jnp.where(row == 0, lows[1], 0.0), s),
            restrict(jnp.where(lane == 0, lows[2], 0.0), s),
        ]
        up = [
            along_x(ups[0], 1),
            restrict(jnp.where(row == 1, ups[1], 0.0), s),
            restrict(jnp.where(lane == 1, ups[2], 0.0), s),
        ]
        return low, up

    def diagonal(lows, ups, spring):
        return lows[0] + lows[1] + lows[2] + ups[0] + ups[1] + ups[2] + spring

    fraction = (den[...].astype(jnp.float32) + 1.0) / BINS
    modulus = 0.05 + 0.95 * fraction * fraction * fraction
    send(0, modulus[None], 1)
    _, xr, _, yr, _, _ = bufs[0]
    row, lane = iota(modulus.shape, 1), iota(modulus.shape, 2)

    def shared(other):
        return jnp.where(other > 0.0, 0.5 * (modulus + other), 0.0)

    wait(0, 0)
    lows = [shared(jnp.concatenate([xr[0, 0], modulus[:-1]], 0))]
    ups = [shared(jnp.concatenate([modulus[1:], xr[1, 0]], 0))]
    wait(0, 1)
    lows.append(shared(jnp.where(row == 0, yr[0, 0], roll(modulus, 1, 1))))
    ups.append(shared(jnp.where(row == ny - 1, yr[1, 0], roll(modulus, -1, 1))))
    beside = z_halo(0, 1)[0]
    lows.append(shared(jnp.where(lane == 0, beside, roll(modulus, 1, 2))))
    ups.append(shared(jnp.where(lane == nz - 1, beside, roll(modulus, -1, 2))))
    spring = 0.1 * modulus

    fixed = fix[...].astype(jnp.float32)
    free_ref[...] = 1.0 - fixed
    diag_ref[...] = free_ref[...] * diagonal(lows, ups, spring) + fixed
    inv_ref[...] = 1.0 / diag_ref[...]
    fc0_ref[...] = damping * res[...] * inv_ref[...]

    masked = free_ref[...] * fc0_ref[...]
    send(1, masked, 1)
    set_coef(0, lows, ups)
    lows, ups = coarse_links(0, lows, ups)
    spring = restrict(spring, 1)
    set_coef(1, lows, ups)
    inv1_ref[...] = 1.0 / diagonal(lows, ups, spring)
    lows, ups = coarse_links(1, lows, ups)
    spring = restrict(spring, 2)
    set_coef(2, lows, ups)
    inv2_ref[...] = 1.0 / diagonal(lows, ups, spring)
    total = halo_sum(0, 1, local_sum(0, masked))
    mid_rhs = restrict((1.0 - damping) * res[...] + free_ref[...] * total, 1)
    mid0 = damping * mid_rhs * inv1_ref[...]
    scaled_rhs = restrict((1.0 - damping) * mid_rhs + neighbours(1, 2, mid0), 2) * inv2_ref[...]

    ratio = eig_center / eig_halfwidth
    factor = 1.0 / ratio
    update = scaled_rhs / eig_center
    iterate = update
    for step in range(SWEEPS - 1):
        remainder = scaled_rhs - iterate + neighbours(2, 3 + step, iterate) * inv2_ref[...]
        next_factor = 1.0 / (2.0 * ratio - factor)
        update = next_factor * factor * update + 2.0 * next_factor / eig_halfwidth * remainder
        iterate = iterate + update
        factor = next_factor

    mid = mid0 + prolong(iterate)
    mid = (1.0 - damping) * mid + mid0 + damping * neighbours(1, 5, mid) * inv1_ref[...]
    fine = fc0_ref[...] + prolong(mid)
    total = neighbours(0, 6, free_ref[...] * fine)
    direction = (
        (1.0 - damping) * fine + fc0_ref[...] + damping * free_ref[...] * total * inv_ref[...]
    )
    out_d[...] = direction
    total = neighbours(0, 7, free_ref[...] * direction)
    direction = out_d[...]
    image = diag_ref[...] * direction - free_ref[...] * total
    out_r[...] = image

    def fold(v):
        w = jnp.sum(v.reshape(-1, 8, nz), axis=0)
        return w + roll(w, 4, 0)

    tile = (8, nz)
    mine = jnp.where(iota(tile, 0) < 4, fold(res[...] * direction), fold(direction * image))

    sent = []
    for a in (2, 1, 0):
        buf = sums[a]
        part[a] = mine
        buf[idx[a]] = mine
        offsets = range(1, counts[a])
        hops = []
        for k in offsets:
            hops.append(
                pltpu.make_async_remote_copy(
                    src_ref=part.at[a],
                    dst_ref=buf.at[idx[a]],
                    send_sem=ssend_sem.at[a, k],
                    recv_sem=srecv_sem.at[a, k],
                    device_id={AXES[a]: lax.rem(idx[a] + k, counts[a])},
                    device_id_type=pl.DeviceIdType.MESH,
                )
            )
            hops[-1].start()
        for k in offsets:
            arrival = pltpu.make_async_remote_copy(
                src_ref=part.at[a],
                dst_ref=buf.at[lax.rem(idx[a] + counts[a] - k, counts[a])],
                send_sem=ssend_sem.at[a, k],
                recv_sem=srecv_sem.at[a, k],
                device_id={AXES[a]: lax.rem(idx[a] + k, counts[a])},
                device_id_type=pl.DeviceIdType.MESH,
            )
            arrival.wait_recv()
        mine = jnp.sum(buf[...], axis=0)
        sent += hops

    def grand(keep):
        picked = jnp.where(keep, mine, 0.0)
        return jnp.sum(jnp.sum(picked, axis=1, keepdims=True), axis=0, keepdims=True)

    head = iota(tile, 0) < 4
    alpha = grand(head) / grand(jnp.logical_not(head))
    out_s[...] = sol[...] + alpha * out_d[...]
    out_r[...] = res[...] - alpha * out_r[...]

    for hop in sent:
        hop.wait_send()
    for r in range(n_rounds):
        for a in range(3):
            to_next, to_prev = copies(r, a)
            pl.when(has_next(a))(to_next.wait_send)
            pl.when(has_prev(a))(to_prev.wait_send)


def shards(counts, solution, residual, density_bins, fixed_dofs):
    comps, nx, ny, nz = residual.shape
    f32 = jnp.float32
    scratch = []
    for level in ROUNDS:
        c, planes = (1, nx) if level == "bins" else (comps, nx // 2**level)
        scratch += [
            pltpu.VMEM((c, planes, ny, nz), f32),
            pltpu.VMEM((2, c, 1, ny, nz), f32),
            pltpu.VMEM((2, c, planes, 1, nz), f32),
            pltpu.VMEM((2, c, planes, 1, nz), f32),
            pltpu.VMEM((ny, nz), f32),
            pltpu.VMEM((2, ny, nz), f32),
        ]
    scratch += [pltpu.VMEM((8, nx // 2**level, ny, nz), f32) for level in range(3)]
    scratch += [pltpu.VMEM((comps, nx, ny, nz), f32)] * 4
    scratch += [pltpu.VMEM((nx // 2, ny, nz), f32), pltpu.VMEM((nx // 4, ny, nz), f32)]
    scratch += [pltpu.VMEM((c, 8, nz), f32) for c in counts]
    scratch += [
        pltpu.VMEM((3, 8, nz), f32),
        pltpu.SemaphoreType.DMA((len(ROUNDS), 6)),
        pltpu.SemaphoreType.DMA((len(ROUNDS), 6)),
        pltpu.SemaphoreType.DMA((3, max(counts))),
        pltpu.SemaphoreType.DMA((3, max(counts))),
    ]
    shape = jax.ShapeDtypeStruct(residual.shape, f32)
    return pl.pallas_call(
        functools.partial(kernel, counts),
        out_shape=(shape, shape, shape),
        in_specs=[pl.BlockSpec(memory_space=pltpu.VMEM)] * 4,
        out_specs=(pl.BlockSpec(memory_space=pltpu.VMEM),) * 3,
        scratch_shapes=scratch,
        compiler_params=pltpu.CompilerParams(
            collective_id=0, has_side_effects=True, vmem_limit_bytes=32 * 2**20
        ),
    )(solution, residual, density_bins, fixed_dofs)


def solution(mesh):
    counts = tuple(mesh.shape[a] for a in AXES)
    return jax.shard_map(
        functools.partial(shards, counts),
        mesh=mesh,
        in_specs=(P(None, *AXES), P(None, *AXES), P(*AXES), P(None, *AXES)),
        out_specs=(P(None, *AXES), P(None, *AXES), P(None, *AXES)),
        check_vma=False,
    )
```

```python
import functools

import jax
import jax.numpy as jnp
from jax import lax
from jax.experimental import pallas as pl
from jax.experimental.pallas import tpu as pltpu
from jax.sharding import PartitionSpec as P

SWEEPS = 3
BINS = 16
AXES = ("gx", "gy", "gz")

damping = 0.6
eig_center = 1.05
eig_halfwidth = 0.95

ROUNDS = ("bins", 0, 1, 2, 2, 1, 0, 0)


def roll(v, shift, axis):
    shift = shift % v.shape[axis]
    return v if shift == 0 else pltpu.roll(v, shift, axis)


def iota(shape, dim):
    return lax.broadcasted_iota(jnp.int32, shape, dim)


def pair_sum(v, s, axis):
    even = (iota(v.shape, axis) // s) % 2 == 0
    return v + jnp.where(even, roll(v, -s, axis), roll(v, s, axis))


def restrict(v, s):
    lead = v.shape[:-3]
    nx, ny, nz = v.shape[-3:]
    w = v.reshape(lead + (nx // 2, 2, ny, nz))
    k = len(lead) + 1
    w = lax.index_in_dim(w, 0, k, False) + lax.index_in_dim(w, 1, k, False)
    return pair_sum(pair_sum(w, s, w.ndim - 2), s, w.ndim - 1)


def prolong(v):
    c, nx, ny, nz = v.shape
    return jnp.broadcast_to(v[:, :, None], (c, nx, 2, ny, nz)).reshape(c, 2 * nx, ny, nz)


def kernel(counts, sol_hbm, res_hbm, den_hbm, fix_hbm, out_s, out_r, out_d, *scratch):
    n_rounds = len(ROUNDS)
    sol, res, den, fix, load_sem = scratch[-5:]
    loads = [
        pltpu.make_async_copy(src, dst, load_sem.at[i])
        for i, (src, dst) in enumerate(
            ((den_hbm, den), (res_hbm, res), (fix_hbm, fix), (sol_hbm, sol))
        )
    ]
    for load in loads:
        load.start()
    bufs = [scratch[6 * r : 6 * r + 6] for r in range(n_rounds)]
    rest = scratch[6 * n_rounds :]
    coef = rest[0:3]
    free_ref, diag_ref, inv_ref, fc0_ref, inv1_ref, inv2_ref = rest[3:9]
    sums = rest[9:12]
    part, send_sem, recv_sem, ssend_sem, srecv_sem = rest[12:17]

    idx = [lax.axis_index(a) for a in AXES]
    ny, nz = den.shape[1:]
    half = ny // 2

    barrier = pltpu.get_barrier_semaphore()
    for a, axis in enumerate(AXES):
        for k in range(1, counts[a]):
            pl.semaphore_signal(
                barrier,
                inc=1,
                device_id={axis: lax.rem(idx[a] + k, counts[a])},
                device_id_type=pl.DeviceIdType.MESH,
            )

    for a in range(3):
        for side, beyond in enumerate((idx[a] == 0, idx[a] == counts[a] - 1)):

            @pl.when(beyond)
            def _():
                for r in range(n_rounds):
                    ref = bufs[r][2 * a + 1]
                    ref[side] = jnp.zeros(ref.shape[1:], jnp.float32)

    def copies(r, a):
        field, xr, ys, yr, zs, zr = bufs[r]
        nx = field.shape[1]
        for up in (0, 1):
            if a == 0:
                src = field.at[:, pl.ds(0 if up else nx - 1, 1)]
                dst = xr.at[up]
            elif a == 1:
                src, dst = ys.at[up], yr.at[up]
            else:
                src, dst = zs, zr.at[up]
            slot = 2 * a + up
            yield pltpu.make_async_remote_copy(
                src_ref=src,
                dst_ref=dst,
                send_sem=send_sem.at[r, slot],
                recv_sem=recv_sem.at[r, slot],
                device_id={AXES[a]: idx[a] - 1 if up else idx[a] + 1},
                device_id_type=pl.DeviceIdType.MESH,
            )

    def has_next(a):
        return idx[a] < counts[a] - 1

    def has_prev(a):
        return idx[a] > 0

    def start(r, a):
        to_next, to_prev = copies(r, a)
        pl.when(has_next(a))(to_next.start)
        pl.when(has_prev(a))(to_prev.start)

    def wait(r, a):
        to_next, to_prev = copies(r, a)
        pl.when(has_prev(a))(to_next.wait_recv)
        pl.when(has_next(a))(to_prev.wait_recv)

    def sent_all(r):
        for a in range(3):
            to_next, to_prev = copies(r, a)
            pl.when(has_next(a))(to_next.wait_send)
            pl.when(has_prev(a))(to_prev.wait_send)

    def send(r, v, s):
        field, xr, ys, yr, zs, zr = bufs[r]
        c, nx = v.shape[:2]
        field[...] = v
        start(r, 0)
        ys[0] = v[:, :, ny - 1 : ny]
        ys[1] = v[:, :, 0:1]
        start(r, 1)
        place = ((iota((ny, nz), 1) + s) % nz) // (2 * s)
        packed = jnp.zeros((ny, nz), jnp.float32)
        for p in range(c * nx):
            packed = jnp.where(place == p, roll(v[p // nx, p % nx], 2 * s * p, 1), packed)
        zs[...] = packed
        start(r, 2)

    def z_halo(r, s):
        field, _, _, _, _, zr = bufs[r]
        c, nx = field.shape[:2]
        wait(r, 2)
        even = (iota((ny, nz), 1) // s) % 2 == 0
        w = jnp.where(even, roll(zr[0], s, 1), roll(zr[1], -s, 1))
        planes = [roll(w, -2 * s * p, 1) for p in range(c * nx)]
        return jnp.stack(planes).reshape(c, nx, ny, nz)

    def set_coef(level, lows, ups):
        ref = coef[level]
        s = 2**level
        shape = lows[0].shape
        row, lane = iota(shape, 1), iota(shape, 2)
        zero = jnp.zeros(shape, jnp.float32)
        ref[0] = lows[0]
        ref[1] = ups[0]
        ref[2] = jnp.where(row >= s, lows[1], zero)
        ref[3] = jnp.where(row < ny - s, ups[1], zero)
        ref[4] = jnp.where(lane >= s, lows[2], zero)
        ref[5] = jnp.where(lane < nz - s, ups[2], zero)
        ref[6] = jnp.where(row < s, lows[1], jnp.where(row >= ny - s, ups[1], zero))
        ref[7] = jnp.where(lane < s, lows[2], jnp.where(lane >= nz - s, ups[2], zero))

    def local_sum(level, v):
        ref = coef[level]
        s = 2**level
        edge = jnp.zeros_like(v[:, :1])
        total = ref[0] * jnp.concatenate([edge, v[:, :-1]], 1)
        total = total + ref[1] * jnp.concatenate([v[:, 1:], edge], 1)
        total = total + ref[2] * roll(v, s, 2) + ref[3] * roll(v, -s, 2)
        return total + ref[4] * roll(v, s, 3) + ref[5] * roll(v, -s, 3)

    def halo_sum(level, r, total):
        ref = coef[level]
        s = 2**level
        _, xr, _, yr, _, _ = bufs[r]
        nx = total.shape[1]
        sent_all(r - 1)
        wait(r, 0)
        first = total[:, :1] + ref[0, 0:1] * xr[0]
        last = total[:, nx - 1 :] + ref[1, nx - 1 : nx] * xr[1]
        middle = [total[:, 1 : nx - 1]] if nx > 2 else []
        total = jnp.concatenate([first] + middle + [last], 1)
        wait(r, 1)
        top = total[:, :, :half] + ref[6, :, :half] * yr[0]
        bottom = total[:, :, half:] + ref[6, :, half:] * yr[1]
        total = jnp.concatenate([top, bottom], 2)
        return total + ref[7] * z_halo(r, s)

    def neighbours(level, r, v):
        send(r, v, 2**level)
        return halo_sum(level, r, local_sum(level, v))

    def coarse_links(level, lows, ups):
        s = 2**level
        nx = lows[0].shape[0]
        row = (iota(lows[0].shape, 1) // s) % 2
        lane = (iota(lows[0].shape, 2) // s) % 2

        def along_x(links, offset):
            w = links.reshape(nx // 2, 2, ny, nz)[:, offset]
            return pair_sum(pair_sum(w, s, 1), s, 2)

        low = [
            along_x(lows[0], 0),
            restrict(jnp.where(row == 0, lows[1], 0.0), s),
            restrict(jnp.where(lane == 0, lows[2], 0.0), s),
        ]
        up = [
            along_x(ups[0], 1),
            restrict(jnp.where(row == 1, ups[1], 0.0), s),
            restrict(jnp.where(lane == 1, ups[2], 0.0), s),
        ]
        return low, up

    def diagonal(lows, ups, spring):
        return lows[0] + lows[1] + lows[2] + ups[0] + ups[1] + ups[2] + spring

    loads[0].wait()
    fraction = (den[...].astype(jnp.float32) + 1.0) / BINS
    modulus = 0.05 + 0.95 * fraction * fraction * fraction
    pl.semaphore_wait(barrier, sum(c - 1 for c in counts))
    send(0, modulus[None], 1)
    _, xr, _, yr, _, _ = bufs[0]
    row, lane = iota(modulus.shape, 1), iota(modulus.shape, 2)

    def shared(other):
        return jnp.where(other > 0.0, 0.5 * (modulus + other), 0.0)

    wait(0, 0)
    lows = [shared(jnp.concatenate([xr[0, 0], modulus[:-1]], 0))]
    ups = [shared(jnp.concatenate([modulus[1:], xr[1, 0]], 0))]
    wait(0, 1)
    lows.append(shared(jnp.where(row == 0, yr[0, 0], roll(modulus, 1, 1))))
    ups.append(shared(jnp.where(row == ny - 1, yr[1, 0], roll(modulus, -1, 1))))
    beside = z_halo(0, 1)[0]
    lows.append(shared(jnp.where(lane == 0, beside, roll(modulus, 1, 2))))
    ups.append(shared(jnp.where(lane == nz - 1, beside, roll(modulus, -1, 2))))
    spring = 0.1 * modulus

    loads[1].wait()
    loads[2].wait()
    fixed = fix[...].astype(jnp.float32)
    free_ref[...] = 1.0 - fixed
    diag_ref[...] = free_ref[...] * diagonal(lows, ups, spring) + fixed
    inv_ref[...] = 1.0 / diag_ref[...]
    fc0_ref[...] = damping * res[...] * inv_ref[...]

    masked = free_ref[...] * fc0_ref[...]
    send(1, masked, 1)
    set_coef(0, lows, ups)
    lows, ups = coarse_links(0, lows, ups)
    spring = restrict(spring, 1)
    set_coef(1, lows, ups)
    inv1_ref[...] = 1.0 / diagonal(lows, ups, spring)
    lows, ups = coarse_links(1, lows, ups)
    spring = restrict(spring, 2)
    set_coef(2, lows, ups)
    inv2_ref[...] = 1.0 / diagonal(lows, ups, spring)
    total = halo_sum(0, 1, local_sum(0, masked))
    mid_rhs = restrict((1.0 - damping) * res[...] + free_ref[...] * total, 1)
    mid0 = damping * mid_rhs * inv1_ref[...]
    scaled_rhs = restrict((1.0 - damping) * mid_rhs + neighbours(1, 2, mid0), 2) * inv2_ref[...]

    ratio = eig_center / eig_halfwidth
    factor = 1.0 / ratio
    update = scaled_rhs / eig_center
    iterate = update
    for step in range(SWEEPS - 1):
        remainder = scaled_rhs - iterate + neighbours(2, 3 + step, iterate) * inv2_ref[...]
        next_factor = 1.0 / (2.0 * ratio - factor)
        update = next_factor * factor * update + 2.0 * next_factor / eig_halfwidth * remainder
        iterate = iterate + update
        factor = next_factor

    mid = mid0 + prolong(iterate)
    mid = (1.0 - damping) * mid + mid0 + damping * neighbours(1, 5, mid) * inv1_ref[...]
    fine = fc0_ref[...] + prolong(mid)
    total = neighbours(0, 6, free_ref[...] * fine)
    direction = (
        (1.0 - damping) * fine + fc0_ref[...] + damping * free_ref[...] * total * inv_ref[...]
    )
    out_d[...] = direction
    total = neighbours(0, 7, free_ref[...] * direction)
    direction = out_d[...]
    image = diag_ref[...] * direction - free_ref[...] * total
    out_r[...] = image

    def fold(v):
        w = jnp.sum(v.reshape(-1, 8, nz), axis=0)
        return w + roll(w, 4, 0)

    tile = (8, nz)
    mine = jnp.where(iota(tile, 0) < 4, fold(res[...] * direction), fold(direction * image))

    sent = []
    for a in (2, 1, 0):
        buf = sums[a]
        part[a] = mine
        buf[idx[a]] = mine
        offsets = range(1, counts[a])
        hops = []
        for k in offsets:
            hops.append(
                pltpu.make_async_remote_copy(
                    src_ref=part.at[a],
                    dst_ref=buf.at[idx[a]],
                    send_sem=ssend_sem.at[a, k],
                    recv_sem=srecv_sem.at[a, k],
                    device_id={AXES[a]: lax.rem(idx[a] + k, counts[a])},
                    device_id_type=pl.DeviceIdType.MESH,
                )
            )
            hops[-1].start()
        for k in offsets:
            arrival = pltpu.make_async_remote_copy(
                src_ref=part.at[a],
                dst_ref=buf.at[lax.rem(idx[a] + counts[a] - k, counts[a])],
                send_sem=ssend_sem.at[a, k],
                recv_sem=srecv_sem.at[a, k],
                device_id={AXES[a]: lax.rem(idx[a] + k, counts[a])},
                device_id_type=pl.DeviceIdType.MESH,
            )
            arrival.wait_recv()
        mine = jnp.sum(buf[...], axis=0)
        sent += hops

    def grand(keep):
        picked = jnp.where(keep, mine, 0.0)
        return jnp.sum(jnp.sum(picked, axis=1, keepdims=True), axis=0, keepdims=True)

    head = iota(tile, 0) < 4
    alpha = grand(head) / grand(jnp.logical_not(head))
    loads[3].wait()
    out_s[...] = sol[...] + alpha * out_d[...]
    out_r[...] = res[...] - alpha * out_r[...]

    for hop in sent:
        hop.wait_send()
    sent_all(n_rounds - 1)


def shards(counts, solution, residual, density_bins, fixed_dofs):
    comps, nx, ny, nz = residual.shape
    f32 = jnp.float32
    scratch = []
    for level in ROUNDS:
        c, planes = (1, nx) if level == "bins" else (comps, nx // 2**level)
        scratch += [
            pltpu.VMEM((c, planes, ny, nz), f32),
            pltpu.VMEM((2, c, 1, ny, nz), f32),
            pltpu.VMEM((2, c, planes, 1, nz), f32),
            pltpu.VMEM((2, c, planes, 1, nz), f32),
            pltpu.VMEM((ny, nz), f32),
            pltpu.VMEM((2, ny, nz), f32),
        ]
    scratch += [pltpu.VMEM((8, nx // 2**level, ny, nz), f32) for level in range(3)]
    scratch += [pltpu.VMEM((comps, nx, ny, nz), f32)] * 4
    scratch += [pltpu.VMEM((nx // 2, ny, nz), f32), pltpu.VMEM((nx // 4, ny, nz), f32)]
    scratch += [pltpu.VMEM((c, 8, nz), f32) for c in counts]
    scratch += [
        pltpu.VMEM((3, 8, nz), f32),
        pltpu.SemaphoreType.DMA((len(ROUNDS), 6)),
        pltpu.SemaphoreType.DMA((len(ROUNDS), 6)),
        pltpu.SemaphoreType.DMA((3, max(counts))),
        pltpu.SemaphoreType.DMA((3, max(counts))),
        pltpu.VMEM(solution.shape, f32),
        pltpu.VMEM(residual.shape, f32),
        pltpu.VMEM(density_bins.shape, jnp.int32),
        pltpu.VMEM(fixed_dofs.shape, jnp.int32),
        pltpu.SemaphoreType.DMA((4,)),
    ]
    operands = [
        pltpu.with_memory_space_constraint(x, pltpu.HBM)
        for x in (solution, residual, density_bins, fixed_dofs)
    ]
    shape = jax.ShapeDtypeStruct(residual.shape, f32)
    return pl.pallas_call(
        functools.partial(kernel, counts),
        out_shape=(shape, shape, shape),
        in_specs=[pl.BlockSpec(memory_space=pltpu.HBM)] * 4,
        out_specs=(pl.BlockSpec(memory_space=pltpu.VMEM),) * 3,
        scratch_shapes=scratch,
        compiler_params=pltpu.CompilerParams(
            collective_id=0, has_side_effects=True, vmem_limit_bytes=32 * 2**20
        ),
    )(*operands)


def solution(mesh):
    counts = tuple(mesh.shape[a] for a in AXES)
    return jax.shard_map(
        functools.partial(shards, counts),
        mesh=mesh,
        in_specs=(P(None, *AXES), P(None, *AXES), P(*AXES), P(None, *AXES)),
        out_specs=(P(None, *AXES), P(None, *AXES), P(None, *AXES)),
        check_vma=False,
    )
```

```python
import functools

import jax
import jax.numpy as jnp
from jax import lax
from jax.experimental import pallas as pl
from jax.experimental.pallas import tpu as pltpu
from jax.sharding import PartitionSpec as P

SWEEPS = 3
BINS = 16
AXES = ("gx", "gy", "gz")

damping = 0.6
eig_center = 1.05
eig_halfwidth = 0.95

ROUNDS = ("bins", 0, 1, 2, 2, 1, 0, 0)


def roll(v, shift, axis):
    shift = shift % v.shape[axis]
    return v if shift == 0 else pltpu.roll(v, shift, axis)


def iota(shape, dim):
    return lax.broadcasted_iota(jnp.int32, shape, dim)


def pair_sum(v, s, axis):
    even = (iota(v.shape, axis) // s) % 2 == 0
    return v + jnp.where(even, roll(v, -s, axis), roll(v, s, axis))


def restrict(v, s):
    lead = v.shape[:-3]
    nx, ny, nz = v.shape[-3:]
    w = v.reshape(lead + (nx // 2, 2, ny, nz))
    k = len(lead) + 1
    w = lax.index_in_dim(w, 0, k, False) + lax.index_in_dim(w, 1, k, False)
    return pair_sum(pair_sum(w, s, w.ndim - 2), s, w.ndim - 1)


def prolong(v):
    c, nx, ny, nz = v.shape
    return jnp.broadcast_to(v[:, :, None], (c, nx, 2, ny, nz)).reshape(c, 2 * nx, ny, nz)


def sum_groups(counts):
    total = counts[0] * counts[1] * counts[2]
    return ((0, 1, 2),) if total <= 64 else ((2,), (1,), (0,))


def group_size(counts, group):
    size = 1
    for a in group:
        size *= counts[a]
    return size


def kernel(counts, sol_hbm, res_hbm, den_hbm, fix_hbm, out_s, out_r, out_d, *scratch):
    n_rounds = len(ROUNDS)
    sol, res, den, fix, load_sem = scratch[-5:]
    loads = [
        pltpu.make_async_copy(src, dst, load_sem.at[i])
        for i, (src, dst) in enumerate(
            ((den_hbm, den), (res_hbm, res), (fix_hbm, fix), (sol_hbm, sol))
        )
    ]
    for load in loads:
        load.start()
    bufs = [scratch[6 * r : 6 * r + 6] for r in range(n_rounds)]
    rest = scratch[6 * n_rounds :]
    coef = rest[0:3]
    free_ref, diag_ref, inv_ref, fc0_ref, inv1_ref, inv2_ref = rest[3:9]
    part, send_sem, recv_sem, ssend_sem, srecv_sem = rest[9:14]
    sums = rest[14:-5]
    groups = sum_groups(counts)

    idx = [lax.axis_index(a) for a in AXES]
    ny, nz = den.shape[1:]
    half = ny // 2

    barrier = pltpu.get_barrier_semaphore()


    def partner(group, k):
        there, place, left = {}, 0, abs(k)
        for a in reversed(group):
            step = left % counts[a]
            left //= counts[a]
            there[a] = lax.rem(idx[a] + (step if k > 0 else counts[a] - step), counts[a])
        for a in group:
            place = place * counts[a] + there[a]
        return {AXES[a]: there[a] for a in group}, place

    greeted = 0
    for group in groups:
        for k in range(1, group_size(counts, group)):
            pl.semaphore_signal(
                barrier,
                inc=1,
                device_id=partner(group, k)[0],
                device_id_type=pl.DeviceIdType.MESH,
            )
            greeted += 1

    for a in range(3):
        for side, beyond in enumerate((idx[a] == 0, idx[a] == counts[a] - 1)):

            @pl.when(beyond)
            def _():
                for r in range(n_rounds):
                    ref = bufs[r][2 * a + 1]
                    ref[side] = jnp.zeros(ref.shape[1:], jnp.float32)

    def copies(r, a):
        field, xr, ys, yr, zs, zr = bufs[r]
        nx = field.shape[1]
        for up in (0, 1):
            if a == 0 and ROUNDS[r] in (1, 2):
                src, dst = field.at[0, up], xr.at[up, 0, 0]
            elif a == 0:
                src = field.at[:, pl.ds(0 if up else nx - 1, 1)]
                dst = xr.at[up]
            elif a == 1:
                src, dst = ys.at[up], yr.at[up]
            else:
                src, dst = zs, zr.at[up]
            slot = 2 * a + up
            yield pltpu.make_async_remote_copy(
                src_ref=src,
                dst_ref=dst,
                send_sem=send_sem.at[r, slot],
                recv_sem=recv_sem.at[r, slot],
                device_id={AXES[a]: idx[a] - 1 if up else idx[a] + 1},
                device_id_type=pl.DeviceIdType.MESH,
            )

    def has_next(a):
        return idx[a] < counts[a] - 1

    def has_prev(a):
        return idx[a] > 0

    def start(r, a):
        to_next, to_prev = copies(r, a)
        pl.when(has_next(a))(to_next.start)
        pl.when(has_prev(a))(to_prev.start)

    def wait(r, a):
        to_next, to_prev = copies(r, a)
        pl.when(has_prev(a))(to_next.wait_recv)
        pl.when(has_next(a))(to_prev.wait_recv)

    def sent_all(r):
        for a in range(3):
            to_next, to_prev = copies(r, a)
            pl.when(has_next(a))(to_next.wait_send)
            pl.when(has_prev(a))(to_prev.wait_send)

    def share(face):
        slot = 2 * (iota(face.shape[1:], 0) % 2) + iota(face.shape[1:], 1) % 2
        out = face[0]
        for k in range(1, face.shape[0]):
            out = jnp.where(slot == k, face[k], out)
        return out

    def unshare(plane, c):
        row, lane = iota(plane.shape, 0) % 2, iota(plane.shape, 1) % 2
        out = []
        for k in range(c):
            i, j = k // 2, k % 2
            w = jnp.where(lane == j, plane, roll(plane, 1 - 2 * j, 1))
            out.append(jnp.where(row == i, w, roll(w, 1 - 2 * i, 0)))
        return jnp.stack(out)[:, None]

    def send(r, v, s):
        field, xr, ys, yr, zs, zr = bufs[r]
        c, nx = v.shape[:2]
        if s == 1:
            field[...] = v
        else:
            field[0, 0] = share(v[:, nx - 1])
            field[0, 1] = share(v[:, 0])
        start(r, 0)
        ys[0] = v[:, :, ny - 1 : ny]
        ys[1] = v[:, :, 0:1]
        start(r, 1)
        place = ((iota((ny, nz), 1) + s) % nz) // (2 * s)
        packed = jnp.zeros((ny, nz), jnp.float32)
        for p in range(c * nx):
            packed = jnp.where(place == p, roll(v[p // nx, p % nx], 2 * s * p, 1), packed)
        zs[...] = packed
        start(r, 2)

    def z_halo(r, s):
        field, _, _, _, _, zr = bufs[r]
        c, nx = field.shape[:2]
        wait(r, 2)
        even = (iota((ny, nz), 1) // s) % 2 == 0
        w = jnp.where(even, roll(zr[0], s, 1), roll(zr[1], -s, 1))
        planes = [roll(w, -2 * s * p, 1) for p in range(c * nx)]
        return jnp.stack(planes).reshape(c, nx, ny, nz)

    def set_coef(level, lows, ups):
        ref = coef[level]
        s = 2**level
        shape = lows[0].shape
        row, lane = iota(shape, 1), iota(shape, 2)
        zero = jnp.zeros(shape, jnp.float32)
        ref[0] = lows[0]
        ref[1] = ups[0]
        ref[2] = jnp.where(row >= s, lows[1], zero)
        ref[3] = jnp.where(row < ny - s, ups[1], zero)
        ref[4] = jnp.where(lane >= s, lows[2], zero)
        ref[5] = jnp.where(lane < nz - s, ups[2], zero)
        ref[6] = jnp.where(row < s, lows[1], jnp.where(row >= ny - s, ups[1], zero))
        ref[7] = jnp.where(lane < s, lows[2], jnp.where(lane >= nz - s, ups[2], zero))

    def local_sum(level, v):
        ref = coef[level]
        s = 2**level
        edge = jnp.zeros_like(v[:, :1])
        total = ref[0] * jnp.concatenate([edge, v[:, :-1]], 1)
        total = total + ref[1] * jnp.concatenate([v[:, 1:], edge], 1)
        total = total + ref[2] * roll(v, s, 2) + ref[3] * roll(v, -s, 2)
        return total + ref[4] * roll(v, s, 3) + ref[5] * roll(v, -s, 3)

    def halo_sum(level, r, total):
        ref = coef[level]
        s = 2**level
        _, xr, _, yr, _, _ = bufs[r]
        nx = total.shape[1]
        sent_all(r - 1)
        wait(r, 0)
        faces = xr if s == 1 else [unshare(xr[i, 0, 0], total.shape[0]) for i in (0, 1)]
        first = total[:, :1] + ref[0, 0:1] * faces[0]
        last = total[:, nx - 1 :] + ref[1, nx - 1 : nx] * faces[1]
        middle = [total[:, 1 : nx - 1]] if nx > 2 else []
        total = jnp.concatenate([first] + middle + [last], 1)
        wait(r, 1)
        top = total[:, :, :half] + ref[6, :, :half] * yr[0]
        bottom = total[:, :, half:] + ref[6, :, half:] * yr[1]
        total = jnp.concatenate([top, bottom], 2)
        return total + ref[7] * z_halo(r, s)

    def neighbours(level, r, v):
        send(r, v, 2**level)
        return halo_sum(level, r, local_sum(level, v))

    def coarse_links(level, lows, ups):
        s = 2**level
        nx = lows[0].shape[0]
        row = (iota(lows[0].shape, 1) // s) % 2
        lane = (iota(lows[0].shape, 2) // s) % 2

        def along_x(links, offset):
            w = links.reshape(nx // 2, 2, ny, nz)[:, offset]
            return pair_sum(pair_sum(w, s, 1), s, 2)

        low = [
            along_x(lows[0], 0),
            restrict(jnp.where(row == 0, lows[1], 0.0), s),
            restrict(jnp.where(lane == 0, lows[2], 0.0), s),
        ]
        up = [
            along_x(ups[0], 1),
            restrict(jnp.where(row == 1, ups[1], 0.0), s),
            restrict(jnp.where(lane == 1, ups[2], 0.0), s),
        ]
        return low, up

    def diagonal(lows, ups, spring):
        return lows[0] + lows[1] + lows[2] + ups[0] + ups[1] + ups[2] + spring

    loads[0].wait()
    fraction = (den[...].astype(jnp.float32) + 1.0) / BINS
    modulus = 0.05 + 0.95 * fraction * fraction * fraction
    pl.semaphore_wait(barrier, greeted)
    send(0, modulus[None], 1)
    _, xr, _, yr, _, _ = bufs[0]
    row, lane = iota(modulus.shape, 1), iota(modulus.shape, 2)

    def shared(other):
        return jnp.where(other > 0.0, 0.5 * (modulus + other), 0.0)

    wait(0, 0)
    lows = [shared(jnp.concatenate([xr[0, 0], modulus[:-1]], 0))]
    ups = [shared(jnp.concatenate([modulus[1:], xr[1, 0]], 0))]
    wait(0, 1)
    lows.append(shared(jnp.where(row == 0, yr[0, 0], roll(modulus, 1, 1))))
    ups.append(shared(jnp.where(row == ny - 1, yr[1, 0], roll(modulus, -1, 1))))
    beside = z_halo(0, 1)[0]
    lows.append(shared(jnp.where(lane == 0, beside, roll(modulus, 1, 2))))
    ups.append(shared(jnp.where(lane == nz - 1, beside, roll(modulus, -1, 2))))
    spring = 0.1 * modulus

    loads[1].wait()
    loads[2].wait()
    fixed = fix[...].astype(jnp.float32)
    free_ref[...] = 1.0 - fixed
    diag_ref[...] = free_ref[...] * diagonal(lows, ups, spring) + fixed
    inv_ref[...] = 1.0 / diag_ref[...]
    fc0_ref[...] = damping * res[...] * inv_ref[...]

    masked = free_ref[...] * fc0_ref[...]
    send(1, masked, 1)
    set_coef(0, lows, ups)
    lows, ups = coarse_links(0, lows, ups)
    spring = restrict(spring, 1)
    set_coef(1, lows, ups)
    inv1_ref[...] = 1.0 / diagonal(lows, ups, spring)
    lows, ups = coarse_links(1, lows, ups)
    spring = restrict(spring, 2)
    set_coef(2, lows, ups)
    inv2_ref[...] = 1.0 / diagonal(lows, ups, spring)
    total = halo_sum(0, 1, local_sum(0, masked))
    mid_rhs = restrict((1.0 - damping) * res[...] + free_ref[...] * total, 1)
    mid0 = damping * mid_rhs * inv1_ref[...]
    scaled_rhs = restrict((1.0 - damping) * mid_rhs + neighbours(1, 2, mid0), 2) * inv2_ref[...]

    ratio = eig_center / eig_halfwidth
    factor = 1.0 / ratio
    update = scaled_rhs / eig_center
    iterate = update
    for step in range(SWEEPS - 1):
        remainder = scaled_rhs - iterate + neighbours(2, 3 + step, iterate) * inv2_ref[...]
        next_factor = 1.0 / (2.0 * ratio - factor)
        update = next_factor * factor * update + 2.0 * next_factor / eig_halfwidth * remainder
        iterate = iterate + update
        factor = next_factor

    mid = mid0 + prolong(iterate)
    mid = (1.0 - damping) * mid + mid0 + damping * neighbours(1, 5, mid) * inv1_ref[...]
    fine = fc0_ref[...] + prolong(mid)
    total = neighbours(0, 6, free_ref[...] * fine)
    direction = (
        (1.0 - damping) * fine + fc0_ref[...] + damping * free_ref[...] * total * inv_ref[...]
    )
    out_d[...] = direction
    total = neighbours(0, 7, free_ref[...] * direction)
    direction = out_d[...]
    image = diag_ref[...] * direction - free_ref[...] * total
    out_r[...] = image

    def fold(v):
        w = jnp.sum(jnp.sum(v.reshape(-1, 8, nz), axis=0), axis=0, keepdims=True)
        return w + roll(w, nz // 2, 1)

    head = iota((1, nz), 1) < nz // 2
    mine = jnp.where(head, fold(res[...] * direction), fold(direction * image))

    sent = []
    for g, group in enumerate(groups):
        buf = sums[g]
        size = group_size(counts, group)
        own = 0
        for a in group:
            own = own * counts[a] + idx[a]
        part[g] = mine
        buf[own] = mine

        def hop(k, slot):
            return pltpu.make_async_remote_copy(
                src_ref=part.at[g],
                dst_ref=buf.at[slot],
                send_sem=ssend_sem.at[g, k],
                recv_sem=srecv_sem.at[g, k],
                device_id=partner(group, k)[0],
                device_id_type=pl.DeviceIdType.MESH,
            )

        hops = [hop(k, own) for k in range(1, size)]
        for h in hops:
            h.start()
        for k in range(1, size):
            hop(k, partner(group, -k)[1]).wait_recv()
        mine = jnp.sum(buf[...], axis=0)
        sent += hops

    def grand(keep):
        return jnp.sum(jnp.where(keep, mine, 0.0), axis=1, keepdims=True)

    alpha = grand(head) / grand(jnp.logical_not(head))
    loads[3].wait()
    out_s[...] = sol[...] + alpha * out_d[...]
    out_r[...] = res[...] - alpha * out_r[...]

    for h in sent:
        h.wait_send()
    sent_all(n_rounds - 1)


def shards(counts, solution, residual, density_bins, fixed_dofs):
    comps, nx, ny, nz = residual.shape
    f32 = jnp.float32
    scratch = []
    for level in ROUNDS:
        c, planes = (1, nx) if level == "bins" else (comps, nx // 2**level)
        scratch += [
            pltpu.VMEM((c, planes, ny, nz), f32),
            pltpu.VMEM((2, c, 1, ny, nz), f32),
            pltpu.VMEM((2, c, planes, 1, nz), f32),
            pltpu.VMEM((2, c, planes, 1, nz), f32),
            pltpu.VMEM((ny, nz), f32),
            pltpu.VMEM((2, ny, nz), f32),
        ]
    scratch += [pltpu.VMEM((8, nx // 2**level, ny, nz), f32) for level in range(3)]
    scratch += [pltpu.VMEM((comps, nx, ny, nz), f32)] * 4
    scratch += [pltpu.VMEM((nx // 2, ny, nz), f32), pltpu.VMEM((nx // 4, ny, nz), f32)]
    sizes = [group_size(counts, g) for g in sum_groups(counts)]
    scratch += [
        pltpu.VMEM((len(sizes), 1, nz), f32),
        pltpu.SemaphoreType.DMA((len(ROUNDS), 6)),
        pltpu.SemaphoreType.DMA((len(ROUNDS), 6)),
        pltpu.SemaphoreType.DMA((len(sizes), max(sizes))),
        pltpu.SemaphoreType.DMA((len(sizes), max(sizes))),
    ]
    scratch += [pltpu.VMEM((size, 1, nz), f32) for size in sizes]
    scratch += [
        pltpu.VMEM(solution.shape, f32),
        pltpu.VMEM(residual.shape, f32),
        pltpu.VMEM(density_bins.shape, jnp.int32),
        pltpu.VMEM(fixed_dofs.shape, jnp.int32),
        pltpu.SemaphoreType.DMA((4,)),
    ]
    operands = [
        pltpu.with_memory_space_constraint(x, pltpu.HBM)
        for x in (solution, residual, density_bins, fixed_dofs)
    ]
    shape = jax.ShapeDtypeStruct(residual.shape, f32)
    return pl.pallas_call(
        functools.partial(kernel, counts),
        out_shape=(shape, shape, shape),
        in_specs=[pl.BlockSpec(memory_space=pltpu.HBM)] * 4,
        out_specs=(pl.BlockSpec(memory_space=pltpu.VMEM),) * 3,
        scratch_shapes=scratch,
        compiler_params=pltpu.CompilerParams(
            collective_id=0, has_side_effects=True, vmem_limit_bytes=32 * 2**20
        ),
    )(*operands)


def solution(mesh):
    counts = tuple(mesh.shape[a] for a in AXES)
    return jax.shard_map(
        functools.partial(shards, counts),
        mesh=mesh,
        in_specs=(P(None, *AXES), P(None, *AXES), P(*AXES), P(None, *AXES)),
        out_specs=(P(None, *AXES), P(None, *AXES), P(None, *AXES)),
        check_vma=False,
    )
```

```python
import functools

import jax
import jax.numpy as jnp
from jax import lax
from jax.experimental import pallas as pl
from jax.experimental.pallas import tpu as pltpu
from jax.sharding import PartitionSpec as P

SWEEPS = 3
BINS = 16
AXES = ("gx", "gy", "gz")

damping = 0.6
eig_center = 1.05
eig_halfwidth = 0.95

ROUNDS = ("bins", 0, 1, 2, 2, 1, 0, 0)


def roll(v, shift, axis):
    shift = shift % v.shape[axis]
    return v if shift == 0 else pltpu.roll(v, shift, axis)


def iota(shape, dim):
    return lax.broadcasted_iota(jnp.int32, shape, dim)


def pair_sum(v, s, axis):
    shape = (1,) * (v.ndim - 2) + v.shape[-2:]
    even = jnp.broadcast_to((iota(shape, axis) & s) == 0, v.shape)
    return v + jnp.where(even, roll(v, -s, axis), roll(v, s, axis))


def restrict(v, s):
    lead = v.shape[:-3]
    nx, ny, nz = v.shape[-3:]
    w = v.reshape(lead + (nx // 2, 2, ny, nz))
    k = len(lead) + 1
    w = lax.index_in_dim(w, 0, k, False) + lax.index_in_dim(w, 1, k, False)
    return pair_sum(pair_sum(w, s, w.ndim - 2), s, w.ndim - 1)


def prolong(v):
    c, nx, ny, nz = v.shape
    return jnp.broadcast_to(v[:, :, None], (c, nx, 2, ny, nz)).reshape(c, 2 * nx, ny, nz)


def sum_groups(counts):
    total = counts[0] * counts[1] * counts[2]
    return ((0, 1, 2),) if total <= 64 else ((2,), (1,), (0,))


def group_size(counts, group):
    size = 1
    for a in group:
        size *= counts[a]
    return size


def kernel(counts, sol_hbm, res_hbm, den_hbm, fix_hbm, out_s, out_r, out_d, *scratch):
    n_rounds = len(ROUNDS)
    sol, res, den, fix, load_sem = scratch[-5:]
    loads = [
        pltpu.make_async_copy(src, dst, load_sem.at[i])
        for i, (src, dst) in enumerate(
            ((den_hbm, den), (res_hbm, res), (fix_hbm, fix), (sol_hbm, sol))
        )
    ]
    for load in loads:
        load.start()
    bufs = [scratch[6 * r : 6 * r + 6] for r in range(n_rounds)]
    rest = scratch[6 * n_rounds :]
    coef = rest[0:3]
    free_ref, diag_ref, inv_ref, fc0_ref, inv1_ref, inv2_ref = rest[3:9]
    part, send_sem, recv_sem, ssend_sem, srecv_sem = rest[9:14]
    sums = rest[14:-5]
    groups = sum_groups(counts)

    idx = [lax.axis_index(a) for a in AXES]
    ny, nz = den.shape[1:]
    half = ny // 2

    barrier = pltpu.get_barrier_semaphore()


    def partner(group, k):
        there, place, left = {}, 0, abs(k)
        for a in reversed(group):
            step = left % counts[a]
            left //= counts[a]
            there[a] = lax.rem(idx[a] + (step if k > 0 else counts[a] - step), counts[a])
        for a in group:
            place = place * counts[a] + there[a]
        return {AXES[a]: there[a] for a in group}, place

    greeted = 0
    for group in groups:
        for k in range(1, group_size(counts, group)):
            pl.semaphore_signal(
                barrier,
                inc=1,
                device_id=partner(group, k)[0],
                device_id_type=pl.DeviceIdType.MESH,
            )
            greeted += 1

    for a in range(3):
        for side, beyond in enumerate((idx[a] == 0, idx[a] == counts[a] - 1)):

            @pl.when(beyond)
            def _():
                for r in range(n_rounds):
                    ref = bufs[r][2 * a + 1]
                    ref[side] = jnp.zeros(ref.shape[1:], jnp.float32)

    def copies(r, a):
        xs, xr, ys, yr, zs, zr = bufs[r]
        for up in (0, 1):
            if a == 0:
                src, dst = xs.at[up], xr.at[up]
            elif a == 1:
                src, dst = ys.at[up], yr.at[up]
            else:
                src, dst = zs, zr.at[up]
            slot = 2 * a + up
            yield pltpu.make_async_remote_copy(
                src_ref=src,
                dst_ref=dst,
                send_sem=send_sem.at[r, slot],
                recv_sem=recv_sem.at[r, slot],
                device_id={AXES[a]: idx[a] - 1 if up else idx[a] + 1},
                device_id_type=pl.DeviceIdType.MESH,
            )

    def has_next(a):
        return idx[a] < counts[a] - 1

    def has_prev(a):
        return idx[a] > 0

    def start(r, a):
        to_next, to_prev = copies(r, a)
        pl.when(has_next(a))(to_next.start)
        pl.when(has_prev(a))(to_prev.start)

    def wait(r, a):
        to_next, to_prev = copies(r, a)
        pl.when(has_prev(a))(to_next.wait_recv)
        pl.when(has_next(a))(to_prev.wait_recv)

    def sent_all(r):
        for a in range(3):
            to_next, to_prev = copies(r, a)
            pl.when(has_next(a))(to_next.wait_send)
            pl.when(has_prev(a))(to_prev.wait_send)

    def share(face):
        slot = 2 * (iota(face.shape[1:], 0) % 2) + iota(face.shape[1:], 1) % 2
        out = face[0]
        for k in range(1, face.shape[0]):
            out = jnp.where(slot == k, face[k], out)
        return out

    def unshare(plane, c):
        row, lane = iota(plane.shape, 0) % 2, iota(plane.shape, 1) % 2
        out = []
        for k in range(c):
            i, j = k // 2, k % 2
            w = jnp.where(lane == j, plane, roll(plane, 1 - 2 * j, 1))
            out.append(jnp.where(row == i, w, roll(w, 1 - 2 * i, 0)))
        return jnp.stack(out)[:, None]

    def send(r, v, s):
        xs, _, ys, _, zs, _ = bufs[r]
        c, nx = v.shape[:2]
        if s == 1:
            xs[0] = v[:, nx - 1]
            xs[1] = v[:, 0]
        else:
            xs[0, 0] = share(v[:, nx - 1])
            xs[1, 0] = share(v[:, 0])
        start(r, 0)
        ys[0] = v[:, :, ny - 1 : ny]
        ys[1] = v[:, :, 0:1]
        start(r, 1)
        place = ((iota((ny, nz), 1) + s) % nz) // (2 * s)
        packed = jnp.zeros((ny, nz), jnp.float32)
        for p in range(c * nx):
            packed = jnp.where(place == p, roll(v[p // nx, p % nx], 2 * s * p, 1), packed)
        zs[...] = packed
        start(r, 2)

    def z_halo(r, s, c, nx):
        zr = bufs[r][5]
        wait(r, 2)
        even = (iota((ny, nz), 1) & s) == 0
        w = jnp.where(even, roll(zr[0], s, 1), roll(zr[1], -s, 1))
        planes = [roll(w, -2 * s * p, 1) for p in range(c * nx)]
        return jnp.stack(planes).reshape(c, nx, ny, nz)

    def set_coef(level, lows, ups):
        ref = coef[level]
        s = 2**level
        row, lane = iota((1, ny, nz), 1), iota((1, ny, nz), 2)
        zero = 0.0
        ref[0] = lows[0]
        ref[1] = ups[0]
        ref[2] = jnp.where(row >= s, lows[1], zero)
        ref[3] = jnp.where(row < ny - s, ups[1], zero)
        ref[4] = jnp.where(lane >= s, lows[2], zero)
        ref[5] = jnp.where(lane < nz - s, ups[2], zero)
        ref[6] = jnp.where(row < s, lows[1], jnp.where(row >= ny - s, ups[1], zero))
        ref[7] = jnp.where(lane < s, lows[2], jnp.where(lane >= nz - s, ups[2], zero))

    def local_sum(level, v):
        ref = coef[level]
        s = 2**level
        edge = jnp.zeros_like(v[:, :1])
        total = ref[0] * jnp.concatenate([edge, v[:, :-1]], 1)
        total = total + ref[1] * jnp.concatenate([v[:, 1:], edge], 1)
        total = total + ref[2] * roll(v, s, 2) + ref[3] * roll(v, -s, 2)
        return total + ref[4] * roll(v, s, 3) + ref[5] * roll(v, -s, 3)

    def halo_sum(level, r, total):
        ref = coef[level]
        s = 2**level
        _, xr, _, yr, _, _ = bufs[r]
        nx = total.shape[1]
        sent_all(r - 1)
        wait(r, 0)
        faces = [xr[i][:, None] if s == 1 else unshare(xr[i, 0], total.shape[0]) for i in (0, 1)]
        first = total[:, :1] + ref[0, 0:1] * faces[0]
        last = total[:, nx - 1 :] + ref[1, nx - 1 : nx] * faces[1]
        middle = [total[:, 1 : nx - 1]] if nx > 2 else []
        total = jnp.concatenate([first] + middle + [last], 1)
        wait(r, 1)
        top = total[:, :, :half] + ref[6, :, :half] * yr[0]
        bottom = total[:, :, half:] + ref[6, :, half:] * yr[1]
        total = jnp.concatenate([top, bottom], 2)
        return total + ref[7] * z_halo(r, s, total.shape[0], nx)

    def neighbours(level, r, v):
        send(r, v, 2**level)
        return halo_sum(level, r, local_sum(level, v))

    def coarse_links(level, lows, ups):
        s = 2**level
        nx = lows[0].shape[0]
        row = iota((1, ny, nz), 1) & s
        lane = iota((1, ny, nz), 2) & s

        def along_x(links, offset):
            w = links.reshape(nx // 2, 2, ny, nz)[:, offset]
            return pair_sum(pair_sum(w, s, 1), s, 2)

        low = [
            along_x(lows[0], 0),
            restrict(jnp.where(row == 0, lows[1], 0.0), s),
            restrict(jnp.where(lane == 0, lows[2], 0.0), s),
        ]
        up = [
            along_x(ups[0], 1),
            restrict(jnp.where(row != 0, ups[1], 0.0), s),
            restrict(jnp.where(lane != 0, ups[2], 0.0), s),
        ]
        return low, up

    def diagonal(lows, ups, spring):
        return lows[0] + lows[1] + lows[2] + ups[0] + ups[1] + ups[2] + spring

    loads[0].wait()
    fraction = (den[...].astype(jnp.float32) + 1.0) / BINS
    modulus = 0.05 + 0.95 * fraction * fraction * fraction
    pl.semaphore_wait(barrier, greeted)
    send(0, modulus[None], 1)
    _, xr, _, yr, _, _ = bufs[0]
    row, lane = iota((1, ny, nz), 1), iota((1, ny, nz), 2)

    def shared(other):
        return jnp.where(other > 0.0, 0.5 * (modulus + other), 0.0)

    wait(0, 0)
    lows = [shared(jnp.concatenate([xr[0], modulus[:-1]], 0))]
    ups = [shared(jnp.concatenate([modulus[1:], xr[1]], 0))]
    wait(0, 1)
    lows.append(shared(jnp.where(row == 0, yr[0, 0], roll(modulus, 1, 1))))
    ups.append(shared(jnp.where(row == ny - 1, yr[1, 0], roll(modulus, -1, 1))))
    beside = z_halo(0, 1, 1, modulus.shape[0])[0]
    lows.append(shared(jnp.where(lane == 0, beside, roll(modulus, 1, 2))))
    ups.append(shared(jnp.where(lane == nz - 1, beside, roll(modulus, -1, 2))))
    spring = 0.1 * modulus

    loads[1].wait()
    loads[2].wait()
    fixed = fix[...].astype(jnp.float32)
    free_ref[...] = 1.0 - fixed
    diag_ref[...] = free_ref[...] * diagonal(lows, ups, spring) + fixed
    inv_ref[...] = 1.0 / diag_ref[...]
    fc0_ref[...] = damping * res[...] * inv_ref[...]

    masked = free_ref[...] * fc0_ref[...]
    send(1, masked, 1)
    set_coef(0, lows, ups)
    total = local_sum(0, masked)
    lows, ups = coarse_links(0, lows, ups)
    spring = restrict(spring, 1)
    inv1_ref[...] = 1.0 / diagonal(lows, ups, spring)
    total = halo_sum(0, 1, total)
    mid_rhs = restrict((1.0 - damping) * res[...] + free_ref[...] * total, 1)
    mid0 = damping * mid_rhs * inv1_ref[...]
    send(2, mid0, 2)
    set_coef(1, lows, ups)
    total = local_sum(1, mid0)
    lows, ups = coarse_links(1, lows, ups)
    spring = restrict(spring, 2)
    set_coef(2, lows, ups)
    inv2_ref[...] = 1.0 / diagonal(lows, ups, spring)
    total = halo_sum(1, 2, total)
    scaled_rhs = restrict((1.0 - damping) * mid_rhs + total, 2) * inv2_ref[...]

    ratio = eig_center / eig_halfwidth
    factor = 1.0 / ratio
    update = scaled_rhs / eig_center
    iterate = update
    for step in range(SWEEPS - 1):
        remainder = scaled_rhs - iterate + neighbours(2, 3 + step, iterate) * inv2_ref[...]
        next_factor = 1.0 / (2.0 * ratio - factor)
        update = next_factor * factor * update + 2.0 * next_factor / eig_halfwidth * remainder
        iterate = iterate + update
        factor = next_factor

    mid = mid0 + prolong(iterate)
    mid = (1.0 - damping) * mid + mid0 + damping * neighbours(1, 5, mid) * inv1_ref[...]
    fine = fc0_ref[...] + prolong(mid)
    total = neighbours(0, 6, free_ref[...] * fine)
    direction = (
        (1.0 - damping) * fine + fc0_ref[...] + damping * free_ref[...] * total * inv_ref[...]
    )
    out_d[...] = direction
    masked = free_ref[...] * direction
    send(7, masked, 1)

    def fold(v):
        w = jnp.sum(jnp.sum(v.reshape(-1, 8, nz), axis=0), axis=0, keepdims=True)
        return w + roll(w, nz // 2, 1)

    precond = fold(res[...] * direction)
    image = diag_ref[...] * direction
    curve = fold(direction * image)
    out_r[...] = image
    total = halo_sum(0, 7, local_sum(0, masked)) * free_ref[...]
    curve = curve - fold(out_d[...] * total)
    out_r[...] = out_r[...] - total
    head = iota((1, nz), 1) < nz // 2
    mine = jnp.where(head, precond, curve)

    sent = []
    for g, group in enumerate(groups):
        buf = sums[g]
        size = group_size(counts, group)
        own = 0
        for a in group:
            own = own * counts[a] + idx[a]
        part[g] = mine
        buf[own] = mine

        def hop(k, slot):
            return pltpu.make_async_remote_copy(
                src_ref=part.at[g],
                dst_ref=buf.at[slot],
                send_sem=ssend_sem.at[g, k],
                recv_sem=srecv_sem.at[g, k],
                device_id=partner(group, k)[0],
                device_id_type=pl.DeviceIdType.MESH,
            )

        hops = [hop(k, own) for k in range(1, size)]
        for h in hops:
            h.start()
        for k in range(1, size):
            hop(k, partner(group, -k)[1]).wait_recv()
        mine = jnp.sum(buf[...], axis=0)
        sent += hops

    def grand(keep):
        return jnp.sum(jnp.where(keep, mine, 0.0), axis=1, keepdims=True)

    alpha = grand(head) / grand(jnp.logical_not(head))
    loads[3].wait()
    out_s[...] = sol[...] + alpha * out_d[...]
    out_r[...] = res[...] - alpha * out_r[...]

    for h in sent:
        h.wait_send()
    sent_all(n_rounds - 1)


def deliver(*refs):
    sem = refs[-1]
    moves = [pltpu.make_async_copy(refs[i], refs[3 + i], sem.at[i]) for i in range(3)]
    for move in moves:
        move.start()
    for move in moves:
        move.wait()


def shards(counts, solution, residual, density_bins, fixed_dofs):
    comps, nx, ny, nz = residual.shape
    f32 = jnp.float32
    scratch = []
    for level in ROUNDS:
        c, planes = (1, nx) if level == "bins" else (comps, nx // 2**level)
        face = 1 if level in (1, 2) else c
        scratch += [
            pltpu.VMEM((2, face, ny, nz), f32),
            pltpu.VMEM((2, face, ny, nz), f32),
            pltpu.VMEM((2, c, planes, 1, nz), f32),
            pltpu.VMEM((2, c, planes, 1, nz), f32),
            pltpu.VMEM((ny, nz), f32),
            pltpu.VMEM((2, ny, nz), f32),
        ]
    scratch += [pltpu.VMEM((8, nx // 2**level, ny, nz), f32) for level in range(3)]
    scratch += [pltpu.VMEM((comps, nx, ny, nz), f32)] * 4
    scratch += [pltpu.VMEM((nx // 2, ny, nz), f32), pltpu.VMEM((nx // 4, ny, nz), f32)]
    sizes = [group_size(counts, g) for g in sum_groups(counts)]
    scratch += [
        pltpu.VMEM((len(sizes), 1, nz), f32),
        pltpu.SemaphoreType.DMA((len(ROUNDS), 6)),
        pltpu.SemaphoreType.DMA((len(ROUNDS), 6)),
        pltpu.SemaphoreType.DMA((len(sizes), max(sizes))),
        pltpu.SemaphoreType.DMA((len(sizes), max(sizes))),
    ]
    scratch += [pltpu.VMEM((size, 1, nz), f32) for size in sizes]
    scratch += [
        pltpu.VMEM(solution.shape, f32),
        pltpu.VMEM(residual.shape, f32),
        pltpu.VMEM(density_bins.shape, jnp.int32),
        pltpu.VMEM(fixed_dofs.shape, jnp.int32),
        pltpu.SemaphoreType.DMA((4,)),
    ]
    operands = [
        pltpu.with_memory_space_constraint(x, pltpu.HBM)
        for x in (solution, residual, density_bins, fixed_dofs)
    ]
    shape = jax.ShapeDtypeStruct(residual.shape, f32)
    results = pl.pallas_call(
        functools.partial(kernel, counts),
        out_shape=(shape, shape, shape),
        in_specs=[pl.BlockSpec(memory_space=pltpu.HBM)] * 4,
        out_specs=(pl.BlockSpec(memory_space=pltpu.VMEM),) * 3,
        scratch_shapes=scratch,
        compiler_params=pltpu.CompilerParams(
            collective_id=0, has_side_effects=True, vmem_limit_bytes=32 * 2**20
        ),
    )(*operands)
    return pl.pallas_call(
        deliver,
        out_shape=(shape, shape, shape),
        in_specs=[pl.BlockSpec(memory_space=pltpu.VMEM)] * 3,
        out_specs=(pl.BlockSpec(memory_space=pltpu.HBM),) * 3,
        scratch_shapes=[pltpu.SemaphoreType.DMA((3,))],
    )(*results)


def solution(mesh):
    counts = tuple(mesh.shape[a] for a in AXES)
    return jax.shard_map(
        functools.partial(shards, counts),
        mesh=mesh,
        in_specs=(P(None, *AXES), P(None, *AXES), P(*AXES), P(None, *AXES)),
        out_specs=(P(None, *AXES), P(None, *AXES), P(None, *AXES)),
        check_vma=False,
    )
```

```python
import functools

import jax
import jax.numpy as jnp
from jax import lax
from jax.experimental import pallas as pl
from jax.experimental.pallas import tpu as pltpu
from jax.sharding import PartitionSpec as P

SWEEPS = 3
BINS = 16
AXES = ("gx", "gy", "gz")

damping = 0.6
eig_center = 1.05
eig_halfwidth = 0.95

ROUNDS = ("bins", 0, 1, 2, 2, 1, 0, 0)


def roll(v, shift, axis):
    shift = shift % v.shape[axis]
    return v if shift == 0 else pltpu.roll(v, shift, axis)


def iota(shape, dim):
    return lax.broadcasted_iota(jnp.int32, shape, dim)


def pair_sum(v, s, axis):
    shape = (1,) * (v.ndim - 2) + v.shape[-2:]
    even = jnp.broadcast_to((iota(shape, axis) & s) == 0, v.shape)
    return v + jnp.where(even, roll(v, -s, axis), roll(v, s, axis))


def restrict(v, s):
    lead = v.shape[:-3]
    nx, ny, nz = v.shape[-3:]
    w = v.reshape(lead + (nx // 2, 2, ny, nz))
    k = len(lead) + 1
    w = lax.index_in_dim(w, 0, k, False) + lax.index_in_dim(w, 1, k, False)
    return pair_sum(pair_sum(w, s, w.ndim - 2), s, w.ndim - 1)


def prolong(v):
    c, nx, ny, nz = v.shape
    return jnp.broadcast_to(v[:, :, None], (c, nx, 2, ny, nz)).reshape(c, 2 * nx, ny, nz)


def sum_groups(counts):
    total = counts[0] * counts[1] * counts[2]
    return ((0, 1, 2),) if total <= 64 else ((2,), (1,), (0,))


def group_size(counts, group):
    size = 1
    for a in group:
        size *= counts[a]
    return size


def kernel(counts, sol_hbm, res_hbm, den_hbm, fix_hbm, out_s, out_r, out_d, *scratch):
    n_rounds = len(ROUNDS)
    sol, res, den, fix, load_sem, field, total_ref, mid_ref = scratch[-8:]
    loads = [
        pltpu.make_async_copy(src, dst, load_sem.at[i])
        for i, (src, dst) in enumerate(
            ((den_hbm, den), (res_hbm, res), (fix_hbm, fix), (sol_hbm, sol))
        )
    ]
    for load in loads:
        load.start()
    bufs = [scratch[6 * r : 6 * r + 6] for r in range(n_rounds)]
    rest = scratch[6 * n_rounds :]
    coef = rest[0:3]
    free_ref, diag_ref, inv_ref, fc0_ref, inv1_ref, inv2_ref = rest[3:9]
    part, send_sem, recv_sem, ssend_sem, srecv_sem = rest[9:14]
    sums = rest[14:-8]
    groups = sum_groups(counts)

    idx = [lax.axis_index(a) for a in AXES]
    comps, nx, ny, nz = res.shape
    half = ny // 2

    barrier = pltpu.get_barrier_semaphore()


    def partner(group, k):
        there, place, left = {}, 0, abs(k)
        for a in reversed(group):
            step = left % counts[a]
            left //= counts[a]
            there[a] = lax.rem(idx[a] + (step if k > 0 else counts[a] - step), counts[a])
        for a in group:
            place = place * counts[a] + there[a]
        return {AXES[a]: there[a] for a in group}, place

    greeted = 0
    for group in groups:
        for k in range(1, group_size(counts, group)):
            pl.semaphore_signal(
                barrier,
                inc=1,
                device_id=partner(group, k)[0],
                device_id_type=pl.DeviceIdType.MESH,
            )
            greeted += 1

    for a in range(3):
        for side, beyond in enumerate((idx[a] == 0, idx[a] == counts[a] - 1)):

            @pl.when(beyond)
            def _():
                for r in range(n_rounds):
                    ref = bufs[r][2 * a + 1]
                    ref[side] = jnp.zeros(ref.shape[1:], jnp.float32)

    def copies(r, a):
        xs, xr, ys, yr, zs, zr = bufs[r]
        for up in (0, 1):
            if a == 0:
                src, dst = xs.at[up], xr.at[up]
            elif a == 1:
                src, dst = ys.at[up], yr.at[up]
            else:
                src, dst = zs, zr.at[up]
            slot = 2 * a + up
            yield pltpu.make_async_remote_copy(
                src_ref=src,
                dst_ref=dst,
                send_sem=send_sem.at[r, slot],
                recv_sem=recv_sem.at[r, slot],
                device_id={AXES[a]: idx[a] - 1 if up else idx[a] + 1},
                device_id_type=pl.DeviceIdType.MESH,
            )

    def has_next(a):
        return idx[a] < counts[a] - 1

    def has_prev(a):
        return idx[a] > 0

    def start(r, a):
        to_next, to_prev = copies(r, a)
        pl.when(has_next(a))(to_next.start)
        pl.when(has_prev(a))(to_prev.start)

    def wait(r, a):
        to_next, to_prev = copies(r, a)
        pl.when(has_prev(a))(to_next.wait_recv)
        pl.when(has_next(a))(to_prev.wait_recv)

    def sent_all(r):
        for a in range(3):
            to_next, to_prev = copies(r, a)
            pl.when(has_next(a))(to_next.wait_send)
            pl.when(has_prev(a))(to_prev.wait_send)

    def share(face):
        slot = 2 * (iota(face.shape[1:], 0) % 2) + iota(face.shape[1:], 1) % 2
        out = face[0]
        for k in range(1, face.shape[0]):
            out = jnp.where(slot == k, face[k], out)
        return out

    def unshare(plane, c):
        row, lane = iota(plane.shape, 0) % 2, iota(plane.shape, 1) % 2
        out = []
        for k in range(c):
            i, j = k // 2, k % 2
            w = jnp.where(lane == j, plane, roll(plane, 1 - 2 * j, 1))
            out.append(jnp.where(row == i, w, roll(w, 1 - 2 * i, 0)))
        return jnp.stack(out)[:, None]

    def send(r, v, s):
        xs, _, ys, _, zs, _ = bufs[r]
        c, nx = v.shape[:2]
        if s == 1:
            xs[0] = v[:, nx - 1]
            xs[1] = v[:, 0]
        else:
            xs[0, 0] = share(v[:, nx - 1])
            xs[1, 0] = share(v[:, 0])
        start(r, 0)
        ys[0] = v[:, :, ny - 1 : ny]
        ys[1] = v[:, :, 0:1]
        start(r, 1)
        place = ((iota((ny, nz), 1) + s) % nz) // (2 * s)
        packed = jnp.zeros((ny, nz), jnp.float32)
        for p in range(c * nx):
            packed = jnp.where(place == p, roll(v[p // nx, p % nx], 2 * s * p, 1), packed)
        zs[...] = packed
        start(r, 2)

    def z_halo(r, s, c, nx):
        zr = bufs[r][5]
        wait(r, 2)
        even = (iota((ny, nz), 1) & s) == 0
        w = jnp.where(even, roll(zr[0], s, 1), roll(zr[1], -s, 1))
        planes = [roll(w, -2 * s * p, 1) for p in range(c * nx)]
        return jnp.stack(planes).reshape(c, nx, ny, nz)

    def per_component(body):
        lax.fori_loop(0, comps, lambda c, _: (body(c), None)[1], None)

    def send_fine(r):
        xs, _, ys, _, zs, _ = bufs[r]
        xs[0] = field[:, nx - 1]
        xs[1] = field[:, 0]
        start(r, 0)
        ys[0] = field[:, :, ny - 1 : ny]
        ys[1] = field[:, :, 0:1]
        start(r, 1)
        place = ((iota((ny, nz), 1) + 1) % nz) // 2

        def pack(c, packed):
            part_c = jnp.zeros((ny, nz), jnp.float32)
            for p in range(nx):
                part_c = jnp.where(place == p, roll(field[c, p], 2 * p, 1), part_c)
            return packed + pltpu.roll(part_c, lax.rem(2 * nx * c, nz), 1)

        zs[...] = lax.fori_loop(0, comps, pack, jnp.zeros((ny, nz), jnp.float32))
        start(r, 2)

    def local_fine():
        def body(c):
            total_ref[c] = local_sum(0, field[pl.ds(c, 1)])[0]

        per_component(body)

    def halo_fine(r):
        _, xr, _, yr, _, zr = bufs[r]
        ref = coef[0]
        sent_all(r - 1)
        for a in range(3):
            wait(r, a)
        even = (iota((ny, nz), 1) & 1) == 0
        beside = jnp.where(even, roll(zr[0], 1, 1), roll(zr[1], -1, 1))

        def one(c):
            w = pltpu.roll(beside, lax.rem(nz - 2 * nx * c, nz), 1)
            z = jnp.stack([roll(w, -2 * p, 1) for p in range(nx)])
            t = total_ref[c] + ref[7] * z
            first = t[:1] + ref[0, 0:1] * xr[0, pl.ds(c, 1)]
            last = t[nx - 1 :] + ref[1, nx - 1 : nx] * xr[1, pl.ds(c, 1)]
            t = jnp.concatenate([first, t[1 : nx - 1], last], 0)
            top = t[:, :half] + ref[6, :, :half] * yr[0, c]
            bottom = t[:, half:] + ref[6, :, half:] * yr[1, c]
            return jnp.concatenate([top, bottom], 1)

        return one

    def set_coef(level, lows, ups):
        ref = coef[level]
        s = 2**level
        row, lane = iota((1, ny, nz), 1), iota((1, ny, nz), 2)
        zero = 0.0
        ref[0] = lows[0]
        ref[1] = ups[0]
        ref[2] = jnp.where(row >= s, lows[1], zero)
        ref[3] = jnp.where(row < ny - s, ups[1], zero)
        ref[4] = jnp.where(lane >= s, lows[2], zero)
        ref[5] = jnp.where(lane < nz - s, ups[2], zero)
        ref[6] = jnp.where(row < s, lows[1], jnp.where(row >= ny - s, ups[1], zero))
        ref[7] = jnp.where(lane < s, lows[2], jnp.where(lane >= nz - s, ups[2], zero))

    def local_sum(level, v):
        ref = coef[level]
        s = 2**level
        edge = jnp.zeros_like(v[:, :1])
        total = ref[0] * jnp.concatenate([edge, v[:, :-1]], 1)
        total = total + ref[1] * jnp.concatenate([v[:, 1:], edge], 1)
        total = total + ref[2] * roll(v, s, 2) + ref[3] * roll(v, -s, 2)
        return total + ref[4] * roll(v, s, 3) + ref[5] * roll(v, -s, 3)

    def halo_sum(level, r, total):
        ref = coef[level]
        s = 2**level
        _, xr, _, yr, _, _ = bufs[r]
        nx = total.shape[1]
        sent_all(r - 1)
        wait(r, 0)
        faces = [xr[i][:, None] if s == 1 else unshare(xr[i, 0], total.shape[0]) for i in (0, 1)]
        first = total[:, :1] + ref[0, 0:1] * faces[0]
        last = total[:, nx - 1 :] + ref[1, nx - 1 : nx] * faces[1]
        middle = [total[:, 1 : nx - 1]] if nx > 2 else []
        total = jnp.concatenate([first] + middle + [last], 1)
        wait(r, 1)
        top = total[:, :, :half] + ref[6, :, :half] * yr[0]
        bottom = total[:, :, half:] + ref[6, :, half:] * yr[1]
        total = jnp.concatenate([top, bottom], 2)
        return total + ref[7] * z_halo(r, s, total.shape[0], nx)

    def neighbours(level, r, v):
        send(r, v, 2**level)
        return halo_sum(level, r, local_sum(level, v))

    def coarse_links(level, lows, ups):
        s = 2**level
        nx = lows[0].shape[0]
        row = iota((1, ny, nz), 1) & s
        lane = iota((1, ny, nz), 2) & s

        def along_x(links, offset):
            w = links.reshape(nx // 2, 2, ny, nz)[:, offset]
            return pair_sum(pair_sum(w, s, 1), s, 2)

        low = [
            along_x(lows[0], 0),
            restrict(jnp.where(row == 0, lows[1], 0.0), s),
            restrict(jnp.where(lane == 0, lows[2], 0.0), s),
        ]
        up = [
            along_x(ups[0], 1),
            restrict(jnp.where(row != 0, ups[1], 0.0), s),
            restrict(jnp.where(lane != 0, ups[2], 0.0), s),
        ]
        return low, up

    def diagonal(lows, ups, spring):
        return lows[0] + lows[1] + lows[2] + ups[0] + ups[1] + ups[2] + spring

    loads[0].wait()
    fraction = (den[...].astype(jnp.float32) + 1.0) / BINS
    modulus = 0.05 + 0.95 * fraction * fraction * fraction
    pl.semaphore_wait(barrier, greeted)
    send(0, modulus[None], 1)
    _, xr, _, yr, _, _ = bufs[0]
    row, lane = iota((1, ny, nz), 1), iota((1, ny, nz), 2)

    def shared(other):
        return jnp.where(other > 0.0, 0.5 * (modulus + other), 0.0)

    wait(0, 0)
    lows = [shared(jnp.concatenate([xr[0], modulus[:-1]], 0))]
    ups = [shared(jnp.concatenate([modulus[1:], xr[1]], 0))]
    wait(0, 1)
    lows.append(shared(jnp.where(row == 0, yr[0, 0], roll(modulus, 1, 1))))
    ups.append(shared(jnp.where(row == ny - 1, yr[1, 0], roll(modulus, -1, 1))))
    beside = z_halo(0, 1, 1, modulus.shape[0])[0]
    lows.append(shared(jnp.where(lane == 0, beside, roll(modulus, 1, 2))))
    ups.append(shared(jnp.where(lane == nz - 1, beside, roll(modulus, -1, 2))))
    spring = 0.1 * modulus

    loads[1].wait()
    loads[2].wait()
    fixed = fix[...].astype(jnp.float32)
    free_ref[...] = 1.0 - fixed
    diag_ref[...] = free_ref[...] * diagonal(lows, ups, spring) + fixed
    inv_ref[...] = 1.0 / diag_ref[...]
    fc0_ref[...] = damping * res[...] * inv_ref[...]

    field[...] = free_ref[...] * fc0_ref[...]
    send_fine(1)
    set_coef(0, lows, ups)
    local_fine()
    lows, ups = coarse_links(0, lows, ups)
    spring = restrict(spring, 1)
    inv1_ref[...] = 1.0 / diagonal(lows, ups, spring)
    neighbour_sum = halo_fine(1)

    def first_residual(c):
        left = (1.0 - damping) * res[c] + free_ref[c] * neighbour_sum(c)
        mid_ref[c] = restrict(left, 1)

    per_component(first_residual)
    mid_rhs = mid_ref[...]
    mid0 = damping * mid_rhs * inv1_ref[...]
    send(2, mid0, 2)
    set_coef(1, lows, ups)
    total = local_sum(1, mid0)
    lows, ups = coarse_links(1, lows, ups)
    spring = restrict(spring, 2)
    set_coef(2, lows, ups)
    inv2_ref[...] = 1.0 / diagonal(lows, ups, spring)
    total = halo_sum(1, 2, total)
    scaled_rhs = restrict((1.0 - damping) * mid_rhs + total, 2) * inv2_ref[...]

    ratio = eig_center / eig_halfwidth
    factor = 1.0 / ratio
    update = scaled_rhs / eig_center
    iterate = update
    for step in range(SWEEPS - 1):
        remainder = scaled_rhs - iterate + neighbours(2, 3 + step, iterate) * inv2_ref[...]
        next_factor = 1.0 / (2.0 * ratio - factor)
        update = next_factor * factor * update + 2.0 * next_factor / eig_halfwidth * remainder
        iterate = iterate + update
        factor = next_factor

    mid = mid0 + prolong(iterate)
    mid = (1.0 - damping) * mid + mid0 + damping * neighbours(1, 5, mid) * inv1_ref[...]
    mid_ref[...] = mid

    def corrected(c):
        return fc0_ref[c] + prolong(mid_ref[pl.ds(c, 1)])[0]

    def mask_corrected(c):
        field[c] = free_ref[c] * corrected(c)

    per_component(mask_corrected)
    send_fine(6)
    local_fine()
    neighbour_sum_2 = halo_fine(6)

    def smooth(c):
        change = damping * free_ref[c] * neighbour_sum_2(c) * inv_ref[c]
        direction = (1.0 - damping) * corrected(c) + fc0_ref[c] + change
        out_d[c] = direction
        field[c] = free_ref[c] * direction

    per_component(smooth)
    send_fine(7)
    local_fine()
    neighbour_sum_3 = halo_fine(7)

    def products(c, sums_so_far):
        direction = out_d[c]
        image = diag_ref[c] * direction - free_ref[c] * neighbour_sum_3(c)
        out_r[c] = image
        both = (res[c] * direction, direction * image)
        return tuple(
            old + jnp.sum(new.reshape(-1, 8, nz), axis=0) for old, new in zip(sums_so_far, both)
        )

    none = jnp.zeros((8, nz), jnp.float32)

    def fold(v):
        w = jnp.sum(v, axis=0, keepdims=True)
        return w + roll(w, nz // 2, 1)

    precond, curve = (fold(v) for v in lax.fori_loop(0, comps, products, (none, none)))
    head = iota((1, nz), 1) < nz // 2
    mine = jnp.where(head, precond, curve)

    for g, group in enumerate(groups):
        buf = sums[g]
        size = group_size(counts, group)
        own = 0
        for a in group:
            own = own * counts[a] + idx[a]
        part[g] = mine
        buf[own] = mine

        def hop(k, slot):
            return pltpu.make_async_remote_copy(
                src_ref=part.at[g],
                dst_ref=buf.at[slot],
                send_sem=ssend_sem.at[g, k],
                recv_sem=srecv_sem.at[g, k],
                device_id=partner(group, k)[0],
                device_id_type=pl.DeviceIdType.MESH,
            )

        hops = [hop(k, own) for k in range(1, size)]
        for h in hops:
            h.start()
        for h in hops:
            h.wait_send()
        for k in range(1, size):
            hop(k, partner(group, -k)[1]).wait_recv()
        mine = jnp.sum(buf[...], axis=0)

    def grand(keep):
        return jnp.sum(jnp.where(keep, mine, 0.0), axis=1, keepdims=True)

    alpha = grand(head) / grand(jnp.logical_not(head))
    loads[3].wait()

    def advance(c):
        out_s[c] = sol[c] + alpha * out_d[c]
        out_r[c] = res[c] - alpha * out_r[c]

    per_component(advance)
    sent_all(n_rounds - 1)


def shards(counts, solution, residual, density_bins, fixed_dofs):
    comps, nx, ny, nz = residual.shape
    f32 = jnp.float32
    scratch = []
    for level in ROUNDS:
        c, planes = (1, nx) if level == "bins" else (comps, nx // 2**level)
        face = 1 if level in (1, 2) else c
        scratch += [
            pltpu.VMEM((2, face, ny, nz), f32),
            pltpu.VMEM((2, face, ny, nz), f32),
            pltpu.VMEM((2, c, planes, 1, nz), f32),
            pltpu.VMEM((2, c, planes, 1, nz), f32),
            pltpu.VMEM((ny, nz), f32),
            pltpu.VMEM((2, ny, nz), f32),
        ]
    scratch += [pltpu.VMEM((8, nx // 2**level, ny, nz), f32) for level in range(3)]
    scratch += [pltpu.VMEM((comps, nx, ny, nz), f32)] * 4
    scratch += [pltpu.VMEM((nx // 2, ny, nz), f32), pltpu.VMEM((nx // 4, ny, nz), f32)]
    sizes = [group_size(counts, g) for g in sum_groups(counts)]
    scratch += [
        pltpu.VMEM((len(sizes), 1, nz), f32),
        pltpu.SemaphoreType.DMA((len(ROUNDS), 6)),
        pltpu.SemaphoreType.DMA((len(ROUNDS), 6)),
        pltpu.SemaphoreType.DMA((len(sizes), max(sizes))),
        pltpu.SemaphoreType.DMA((len(sizes), max(sizes))),
    ]
    scratch += [pltpu.VMEM((size, 1, nz), f32) for size in sizes]
    scratch += [
        pltpu.VMEM(solution.shape, f32),
        pltpu.VMEM(residual.shape, f32),
        pltpu.VMEM(density_bins.shape, jnp.int32),
        pltpu.VMEM(fixed_dofs.shape, jnp.int32),
        pltpu.SemaphoreType.DMA((4,)),
        pltpu.VMEM(residual.shape, f32),
        pltpu.VMEM(residual.shape, f32),
        pltpu.VMEM((comps, nx // 2, ny, nz), f32),
    ]
    operands = [
        pltpu.with_memory_space_constraint(x, pltpu.HBM)
        for x in (solution, residual, density_bins, fixed_dofs)
    ]
    shape = jax.ShapeDtypeStruct(residual.shape, f32)
    return pl.pallas_call(
        functools.partial(kernel, counts),
        out_shape=(shape, shape, shape),
        in_specs=[pl.BlockSpec(memory_space=pltpu.HBM)] * 4,
        out_specs=(pl.BlockSpec(memory_space=pltpu.VMEM),) * 3,
        scratch_shapes=scratch,
        compiler_params=pltpu.CompilerParams(
            collective_id=0, has_side_effects=True, vmem_limit_bytes=32 * 2**20
        ),
    )(*operands)


def solution(mesh):
    counts = tuple(mesh.shape[a] for a in AXES)
    return jax.shard_map(
        functools.partial(shards, counts),
        mesh=mesh,
        in_specs=(P(None, *AXES), P(None, *AXES), P(*AXES), P(None, *AXES)),
        out_specs=(P(None, *AXES), P(None, *AXES), P(None, *AXES)),
        check_vma=False,
    )
```

```python
import functools

import jax
import jax.numpy as jnp
from jax import lax
from jax.experimental import pallas as pl
from jax.experimental.pallas import tpu as pltpu
from jax.sharding import PartitionSpec as P

SWEEPS = 3
BINS = 16
AXES = ("gx", "gy", "gz")

damping = 0.6
eig_center = 1.05
eig_halfwidth = 0.95

ROUNDS = ("bins", 0, 1, 2, 2, 1, 0, 0)


def roll(v, shift, axis):
    shift = shift % v.shape[axis]
    return v if shift == 0 else pltpu.roll(v, shift, axis)


def iota(shape, dim):
    return lax.broadcasted_iota(jnp.int32, shape, dim)


def pair_sum(v, s, axis):
    shape = (1,) * (v.ndim - 2) + v.shape[-2:]
    even = jnp.broadcast_to((iota(shape, axis) & s) == 0, v.shape)
    return v + jnp.where(even, roll(v, -s, axis), roll(v, s, axis))


def restrict(v, s):
    lead = v.shape[:-3]
    nx, ny, nz = v.shape[-3:]
    w = v.reshape(lead + (nx // 2, 2, ny, nz))
    k = len(lead) + 1
    w = lax.index_in_dim(w, 0, k, False) + lax.index_in_dim(w, 1, k, False)
    return pair_sum(pair_sum(w, s, w.ndim - 2), s, w.ndim - 1)


def prolong(v):
    c, nx, ny, nz = v.shape
    return jnp.broadcast_to(v[:, :, None], (c, nx, 2, ny, nz)).reshape(c, 2 * nx, ny, nz)


def sum_groups(counts):
    total = counts[0] * counts[1] * counts[2]
    return ((0, 1, 2),) if total <= 64 else ((2,), (1,), (0,))


def group_size(counts, group):
    size = 1
    for a in group:
        size *= counts[a]
    return size


def kernel(counts, res_hbm, den_hbm, fix_hbm, out_r, out_b, out_c, out_a, *scratch):
    n_rounds = len(ROUNDS)
    res, den, fix, load_sem = scratch[-4:]
    loads = [
        pltpu.make_async_copy(src, dst, load_sem.at[i])
        for i, (src, dst) in enumerate(
            ((den_hbm, den), (res_hbm, res), (fix_hbm, fix))
        )
    ]
    for load in loads:
        load.start()
    bufs = [scratch[6 * r : 6 * r + 6] for r in range(n_rounds)]
    rest = scratch[6 * n_rounds :]
    coef = rest[0:3]
    free_ref, diag_ref, inv_ref, fc0_ref, inv1_ref, inv2_ref = rest[3:9]
    part, send_sem, recv_sem, ssend_sem, srecv_sem = rest[9:14]
    sums = rest[14:-4]
    groups = sum_groups(counts)

    idx = [lax.axis_index(a) for a in AXES]
    ny, nz = den.shape[1:]
    half = ny // 2

    barrier = pltpu.get_barrier_semaphore()


    def partner(group, k):
        there, place, left = {}, 0, abs(k)
        for a in reversed(group):
            step = left % counts[a]
            left //= counts[a]
            there[a] = lax.rem(idx[a] + (step if k > 0 else counts[a] - step), counts[a])
        for a in group:
            place = place * counts[a] + there[a]
        return {AXES[a]: there[a] for a in group}, place

    greeted = 0
    for group in groups:
        for k in range(1, group_size(counts, group)):
            pl.semaphore_signal(
                barrier,
                inc=1,
                device_id=partner(group, k)[0],
                device_id_type=pl.DeviceIdType.MESH,
            )
            greeted += 1

    for a in range(3):
        for side, beyond in enumerate((idx[a] == 0, idx[a] == counts[a] - 1)):

            @pl.when(beyond)
            def _():
                for r in range(n_rounds):
                    ref = bufs[r][2 * a + 1]
                    ref[side] = jnp.zeros(ref.shape[1:], jnp.float32)

    def copies(r, a):
        xs, xr, ys, yr, zs, zr = bufs[r]
        for up in (0, 1):
            if a == 0:
                src, dst = xs.at[up], xr.at[up]
            elif a == 1:
                src, dst = ys.at[up], yr.at[up]
            else:
                src, dst = zs, zr.at[up]
            slot = 2 * a + up
            yield pltpu.make_async_remote_copy(
                src_ref=src,
                dst_ref=dst,
                send_sem=send_sem.at[r, slot],
                recv_sem=recv_sem.at[r, slot],
                device_id={AXES[a]: idx[a] - 1 if up else idx[a] + 1},
                device_id_type=pl.DeviceIdType.MESH,
            )

    def has_next(a):
        return idx[a] < counts[a] - 1

    def has_prev(a):
        return idx[a] > 0

    def start(r, a):
        to_next, to_prev = copies(r, a)
        pl.when(has_next(a))(to_next.start)
        pl.when(has_prev(a))(to_prev.start)

    def wait(r, a):
        to_next, to_prev = copies(r, a)
        pl.when(has_prev(a))(to_next.wait_recv)
        pl.when(has_next(a))(to_prev.wait_recv)

    def sent_all(r):
        for a in range(3):
            to_next, to_prev = copies(r, a)
            pl.when(has_next(a))(to_next.wait_send)
            pl.when(has_prev(a))(to_prev.wait_send)

    def share(face):
        slot = 2 * (iota(face.shape[1:], 0) % 2) + iota(face.shape[1:], 1) % 2
        out = face[0]
        for k in range(1, face.shape[0]):
            out = jnp.where(slot == k, face[k], out)
        return out

    def unshare(plane, c):
        row, lane = iota(plane.shape, 0) % 2, iota(plane.shape, 1) % 2
        out = []
        for k in range(c):
            i, j = k // 2, k % 2
            w = jnp.where(lane == j, plane, roll(plane, 1 - 2 * j, 1))
            out.append(jnp.where(row == i, w, roll(w, 1 - 2 * i, 0)))
        return jnp.stack(out)[:, None]

    def send(r, v, s):
        xs, _, ys, _, zs, _ = bufs[r]
        c, nx = v.shape[:2]
        if s == 1:
            xs[0] = v[:, nx - 1]
            xs[1] = v[:, 0]
        else:
            xs[0, 0] = share(v[:, nx - 1])
            xs[1, 0] = share(v[:, 0])
        start(r, 0)
        ys[0] = v[:, :, ny - 1 : ny]
        ys[1] = v[:, :, 0:1]
        start(r, 1)
        place = ((iota((ny, nz), 1) + s) % nz) // (2 * s)
        packed = jnp.zeros((ny, nz), jnp.float32)
        for p in range(c * nx):
            packed = jnp.where(place == p, roll(v[p // nx, p % nx], 2 * s * p, 1), packed)
        zs[...] = packed
        start(r, 2)

    def z_halo(r, s, c, nx):
        zr = bufs[r][5]
        wait(r, 2)
        even = (iota((ny, nz), 1) & s) == 0
        w = jnp.where(even, roll(zr[0], s, 1), roll(zr[1], -s, 1))
        planes = [roll(w, -2 * s * p, 1) for p in range(c * nx)]
        return jnp.stack(planes).reshape(c, nx, ny, nz)

    def set_coef(level, lows, ups):
        ref = coef[level]
        s = 2**level
        row, lane = iota((1, ny, nz), 1), iota((1, ny, nz), 2)
        zero = 0.0
        ref[0] = lows[0]
        ref[1] = ups[0]
        ref[2] = jnp.where(row >= s, lows[1], zero)
        ref[3] = jnp.where(row < ny - s, ups[1], zero)
        ref[4] = jnp.where(lane >= s, lows[2], zero)
        ref[5] = jnp.where(lane < nz - s, ups[2], zero)
        ref[6] = jnp.where(row < s, lows[1], jnp.where(row >= ny - s, ups[1], zero))
        ref[7] = jnp.where(lane < s, lows[2], jnp.where(lane >= nz - s, ups[2], zero))

    def local_sum(level, v):
        ref = coef[level]
        s = 2**level
        edge = jnp.zeros_like(v[:, :1])
        total = ref[0] * jnp.concatenate([edge, v[:, :-1]], 1)
        total = total + ref[1] * jnp.concatenate([v[:, 1:], edge], 1)
        total = total + ref[2] * roll(v, s, 2) + ref[3] * roll(v, -s, 2)
        return total + ref[4] * roll(v, s, 3) + ref[5] * roll(v, -s, 3)

    def halo_sum(level, r, total):
        ref = coef[level]
        s = 2**level
        _, xr, _, yr, _, _ = bufs[r]
        nx = total.shape[1]
        sent_all(r - 1)
        wait(r, 0)
        faces = [xr[i][:, None] if s == 1 else unshare(xr[i, 0], total.shape[0]) for i in (0, 1)]
        first = total[:, :1] + ref[0, 0:1] * faces[0]
        last = total[:, nx - 1 :] + ref[1, nx - 1 : nx] * faces[1]
        middle = [total[:, 1 : nx - 1]] if nx > 2 else []
        total = jnp.concatenate([first] + middle + [last], 1)
        wait(r, 1)
        top = total[:, :, :half] + ref[6, :, :half] * yr[0]
        bottom = total[:, :, half:] + ref[6, :, half:] * yr[1]
        total = jnp.concatenate([top, bottom], 2)
        return total + ref[7] * z_halo(r, s, total.shape[0], nx)

    def neighbours(level, r, v):
        send(r, v, 2**level)
        return halo_sum(level, r, local_sum(level, v))

    def coarse_links(level, lows, ups):
        s = 2**level
        nx = lows[0].shape[0]
        row = iota((1, ny, nz), 1) & s
        lane = iota((1, ny, nz), 2) & s

        def along_x(links, offset):
            w = links.reshape(nx // 2, 2, ny, nz)[:, offset]
            return pair_sum(pair_sum(w, s, 1), s, 2)

        low = [
            along_x(lows[0], 0),
            restrict(jnp.where(row == 0, lows[1], 0.0), s),
            restrict(jnp.where(lane == 0, lows[2], 0.0), s),
        ]
        up = [
            along_x(ups[0], 1),
            restrict(jnp.where(row != 0, ups[1], 0.0), s),
            restrict(jnp.where(lane != 0, ups[2], 0.0), s),
        ]
        return low, up

    def diagonal(lows, ups, spring):
        return lows[0] + lows[1] + lows[2] + ups[0] + ups[1] + ups[2] + spring

    loads[0].wait()
    fraction = (den[...].astype(jnp.float32) + 1.0) / BINS
    modulus = 0.05 + 0.95 * fraction * fraction * fraction
    pl.semaphore_wait(barrier, greeted)
    send(0, modulus[None], 1)
    _, xr, _, yr, _, _ = bufs[0]
    row, lane = iota((1, ny, nz), 1), iota((1, ny, nz), 2)

    def shared(other):
        return jnp.where(other > 0.0, 0.5 * (modulus + other), 0.0)

    wait(0, 0)
    lows = [shared(jnp.concatenate([xr[0], modulus[:-1]], 0))]
    ups = [shared(jnp.concatenate([modulus[1:], xr[1]], 0))]
    wait(0, 1)
    lows.append(shared(jnp.where(row == 0, yr[0, 0], roll(modulus, 1, 1))))
    ups.append(shared(jnp.where(row == ny - 1, yr[1, 0], roll(modulus, -1, 1))))
    beside = z_halo(0, 1, 1, modulus.shape[0])[0]
    lows.append(shared(jnp.where(lane == 0, beside, roll(modulus, 1, 2))))
    ups.append(shared(jnp.where(lane == nz - 1, beside, roll(modulus, -1, 2))))
    spring = 0.1 * modulus

    loads[1].wait()
    loads[2].wait()
    fixed = fix[...].astype(jnp.float32)
    free_ref[...] = 1.0 - fixed
    diag_ref[...] = free_ref[...] * diagonal(lows, ups, spring) + fixed
    inv_ref[...] = 1.0 / diag_ref[...]
    fc0_ref[...] = damping * res[...] * inv_ref[...]

    masked = free_ref[...] * fc0_ref[...]
    send(1, masked, 1)
    set_coef(0, lows, ups)
    total = local_sum(0, masked)
    lows, ups = coarse_links(0, lows, ups)
    spring = restrict(spring, 1)
    inv1_ref[...] = 1.0 / diagonal(lows, ups, spring)
    total = halo_sum(0, 1, total)
    mid_rhs = restrict((1.0 - damping) * res[...] + free_ref[...] * total, 1)
    mid0 = damping * mid_rhs * inv1_ref[...]
    send(2, mid0, 2)
    set_coef(1, lows, ups)
    total = local_sum(1, mid0)
    lows, ups = coarse_links(1, lows, ups)
    spring = restrict(spring, 2)
    set_coef(2, lows, ups)
    inv2_ref[...] = 1.0 / diagonal(lows, ups, spring)
    total = halo_sum(1, 2, total)
    scaled_rhs = restrict((1.0 - damping) * mid_rhs + total, 2) * inv2_ref[...]

    ratio = eig_center / eig_halfwidth
    factor = 1.0 / ratio
    update = scaled_rhs / eig_center
    iterate = update
    for step in range(SWEEPS - 1):
        remainder = scaled_rhs - iterate + neighbours(2, 3 + step, iterate) * inv2_ref[...]
        next_factor = 1.0 / (2.0 * ratio - factor)
        update = next_factor * factor * update + 2.0 * next_factor / eig_halfwidth * remainder
        iterate = iterate + update
        factor = next_factor

    mid = mid0 + prolong(iterate)
    mid = (1.0 - damping) * mid + mid0 + damping * neighbours(1, 5, mid) * inv1_ref[...]
    fine = fc0_ref[...] + prolong(mid)
    total = neighbours(0, 6, free_ref[...] * fine)
    base = (1.0 - damping) * fine + fc0_ref[...]
    change = damping * free_ref[...] * total * inv_ref[...]
    out_b[...] = base
    out_c[...] = change
    direction = base + change
    masked = free_ref[...] * direction
    send(7, masked, 1)

    def fold(v):
        w = jnp.sum(jnp.sum(v.reshape(-1, 8, nz), axis=0), axis=0, keepdims=True)
        return w + roll(w, nz // 2, 1)

    precond = fold(res[...] * direction)
    image = diag_ref[...] * direction
    curve = fold(direction * image)
    out_r[...] = image
    total = halo_sum(0, 7, local_sum(0, masked)) * free_ref[...]
    curve = curve - fold((out_b[...] + out_c[...]) * total)
    out_r[...] = out_r[...] - total
    head = iota((1, nz), 1) < nz // 2
    mine = jnp.where(head, precond, curve)

    sent_all(n_rounds - 1)

    for g, group in enumerate(groups):
        buf = sums[g]
        size = group_size(counts, group)
        own = 0
        for a in group:
            own = own * counts[a] + idx[a]
        part[g] = mine
        buf[own] = mine

        def hop(k, slot):
            return pltpu.make_async_remote_copy(
                src_ref=part.at[g],
                dst_ref=buf.at[slot],
                send_sem=ssend_sem.at[g, k],
                recv_sem=srecv_sem.at[g, k],
                device_id=partner(group, k)[0],
                device_id_type=pl.DeviceIdType.MESH,
            )

        hops = [hop(k, own) for k in range(1, size)]
        for h in hops:
            h.start()
        for h in hops:
            h.wait_send()
        for k in range(1, size):
            hop(k, partner(group, -k)[1]).wait_recv()
        mine = jnp.sum(buf[...], axis=0)

    def grand(keep):
        return jnp.sum(jnp.where(keep, mine, 0.0), axis=1, keepdims=True)

    alpha = grand(head) / grand(jnp.logical_not(head))
    out_a[...] = jnp.broadcast_to(alpha, out_a.shape)


def shards(counts, solution, residual, density_bins, fixed_dofs):
    comps, nx, ny, nz = residual.shape
    f32 = jnp.float32
    scratch = []
    for level in ROUNDS:
        c, planes = (1, nx) if level == "bins" else (comps, nx // 2**level)
        face = 1 if level in (1, 2) else c
        scratch += [
            pltpu.VMEM((2, face, ny, nz), f32),
            pltpu.VMEM((2, face, ny, nz), f32),
            pltpu.VMEM((2, c, planes, 1, nz), f32),
            pltpu.VMEM((2, c, planes, 1, nz), f32),
            pltpu.VMEM((ny, nz), f32),
            pltpu.VMEM((2, ny, nz), f32),
        ]
    scratch += [pltpu.VMEM((8, nx // 2**level, ny, nz), f32) for level in range(3)]
    scratch += [pltpu.VMEM((comps, nx, ny, nz), f32)] * 4
    scratch += [pltpu.VMEM((nx // 2, ny, nz), f32), pltpu.VMEM((nx // 4, ny, nz), f32)]
    sizes = [group_size(counts, g) for g in sum_groups(counts)]
    scratch += [
        pltpu.VMEM((len(sizes), 1, nz), f32),
        pltpu.SemaphoreType.DMA((len(ROUNDS), 6)),
        pltpu.SemaphoreType.DMA((len(ROUNDS), 6)),
        pltpu.SemaphoreType.DMA((len(sizes), max(sizes))),
        pltpu.SemaphoreType.DMA((len(sizes), max(sizes))),
    ]
    scratch += [pltpu.VMEM((size, 1, nz), f32) for size in sizes]
    scratch += [
        pltpu.VMEM(residual.shape, f32),
        pltpu.VMEM(density_bins.shape, jnp.int32),
        pltpu.VMEM(fixed_dofs.shape, jnp.int32),
        pltpu.SemaphoreType.DMA((3,)),
    ]
    operands = [
        pltpu.with_memory_space_constraint(x, pltpu.HBM)
        for x in (residual, density_bins, fixed_dofs)
    ]
    shape = jax.ShapeDtypeStruct(residual.shape, f32)
    image, base, change, alpha = pl.pallas_call(
        functools.partial(kernel, counts),
        out_shape=(shape, shape, shape, jax.ShapeDtypeStruct((1, nz), f32)),
        in_specs=[pl.BlockSpec(memory_space=pltpu.HBM)] * 3,
        out_specs=(pl.BlockSpec(memory_space=pltpu.VMEM),) * 4,
        scratch_shapes=scratch,
        compiler_params=pltpu.CompilerParams(
            collective_id=0, has_side_effects=True, vmem_limit_bytes=32 * 2**20
        ),
    )(*operands)
    direction = base + change
    return (solution + alpha * direction, residual - alpha * image, direction)


def solution(mesh):
    counts = tuple(mesh.shape[a] for a in AXES)
    return jax.shard_map(
        functools.partial(shards, counts),
        mesh=mesh,
        in_specs=(P(None, *AXES), P(None, *AXES), P(*AXES), P(None, *AXES)),
        out_specs=(P(None, *AXES), P(None, *AXES), P(None, *AXES)),
        check_vma=False,
    )
```

```python
import functools

import jax
import jax.numpy as jnp
from jax import lax
from jax.experimental import pallas as pl
from jax.experimental.pallas import tpu as pltpu
from jax.sharding import PartitionSpec as P

SWEEPS = 3
BINS = 16
AXES = ("gx", "gy", "gz")

damping = 0.6
eig_center = 1.05
eig_halfwidth = 0.95

ROUNDS = ("bins", 0, 1, 2, 2, 1, 0, 0)


def roll(v, shift, axis):
    shift = shift % v.shape[axis]
    return v if shift == 0 else pltpu.roll(v, shift, axis)


def iota(shape, dim):
    return lax.broadcasted_iota(jnp.int32, shape, dim)


def pair_sum(v, s, axis):
    shape = (1,) * (v.ndim - 2) + v.shape[-2:]
    even = jnp.broadcast_to((iota(shape, axis) & s) == 0, v.shape)
    return v + jnp.where(even, roll(v, -s, axis), roll(v, s, axis))


def restrict(v, s):
    lead = v.shape[:-3]
    nx, ny, nz = v.shape[-3:]
    w = v.reshape(lead + (nx // 2, 2, ny, nz))
    k = len(lead) + 1
    w = lax.index_in_dim(w, 0, k, False) + lax.index_in_dim(w, 1, k, False)
    return pair_sum(pair_sum(w, s, w.ndim - 2), s, w.ndim - 1)


def prolong(v):
    c, nx, ny, nz = v.shape
    return jnp.broadcast_to(v[:, :, None], (c, nx, 2, ny, nz)).reshape(c, 2 * nx, ny, nz)


def sum_groups(counts):
    total = counts[0] * counts[1] * counts[2]
    return ((0, 1, 2),) if total <= 64 else ((2,), (1,), (0,))


def group_size(counts, group):
    size = 1
    for a in group:
        size *= counts[a]
    return size


def kernel(counts, res_hbm, den_hbm, fix_hbm, out_r, out_b, out_c, out_a, *scratch):
    n_rounds = len(ROUNDS)
    res, den, fix, load_sem = scratch[-4:]
    loads = [
        pltpu.make_async_copy(src, dst, load_sem.at[i])
        for i, (src, dst) in enumerate(
            ((den_hbm, den), (res_hbm, res), (fix_hbm, fix))
        )
    ]
    for load in loads:
        load.start()
    bufs = [scratch[6 * r : 6 * r + 6] for r in range(n_rounds)]
    rest = scratch[6 * n_rounds :]
    coef = rest[0:3]
    free_ref, diag_ref, inv_ref, fc0_ref, inv1_ref, inv2_ref = rest[3:9]
    part, send_sem, recv_sem, ssend_sem, srecv_sem = rest[9:14]
    sums = rest[14:-4]
    groups = sum_groups(counts)

    idx = [lax.axis_index(a) for a in AXES]
    ny, nz = den.shape[1:]
    half = ny // 2

    barrier = pltpu.get_barrier_semaphore()


    def partner(group, k):
        there, place, left = {}, 0, abs(k)
        for a in reversed(group):
            step = left % counts[a]
            left //= counts[a]
            there[a] = lax.rem(idx[a] + (step if k > 0 else counts[a] - step), counts[a])
        for a in group:
            place = place * counts[a] + there[a]
        return {AXES[a]: there[a] for a in group}, place

    greeted = 0
    for group in groups:
        for k in range(1, group_size(counts, group)):
            pl.semaphore_signal(
                barrier,
                inc=1,
                device_id=partner(group, k)[0],
                device_id_type=pl.DeviceIdType.MESH,
            )
            greeted += 1

    for a in range(3):
        for side, beyond in enumerate((idx[a] == 0, idx[a] == counts[a] - 1)):

            @pl.when(beyond)
            def _():
                for r in range(n_rounds):
                    ref = bufs[r][2 * a + 1]
                    ref[side] = jnp.zeros(ref.shape[1:], jnp.float32)

    def copies(r, a):
        xs, xr, ys, yr, zs, zr = bufs[r]
        for up in (0, 1):
            if a == 0:
                src, dst = xs.at[up], xr.at[up]
            elif a == 1:
                src, dst = ys.at[up], yr.at[up]
            else:
                src, dst = zs, zr.at[up]
            slot = 2 * a + up
            yield pltpu.make_async_remote_copy(
                src_ref=src,
                dst_ref=dst,
                send_sem=send_sem.at[r, slot],
                recv_sem=recv_sem.at[r, slot],
                device_id={AXES[a]: idx[a] - 1 if up else idx[a] + 1},
                device_id_type=pl.DeviceIdType.MESH,
            )

    def has_next(a):
        return idx[a] < counts[a] - 1

    def has_prev(a):
        return idx[a] > 0

    def start(r, a):
        to_next, to_prev = copies(r, a)
        pl.when(has_next(a))(to_next.start)
        pl.when(has_prev(a))(to_prev.start)

    def wait(r, a):
        to_next, to_prev = copies(r, a)
        pl.when(has_prev(a))(to_next.wait_recv)
        pl.when(has_next(a))(to_prev.wait_recv)

    def sent_all(r):
        for a in range(3):
            to_next, to_prev = copies(r, a)
            pl.when(has_next(a))(to_next.wait_send)
            pl.when(has_prev(a))(to_prev.wait_send)

    def share(face):
        slot = 2 * (iota(face.shape[1:], 0) % 2) + iota(face.shape[1:], 1) % 2
        out = face[0]
        for k in range(1, face.shape[0]):
            out = jnp.where(slot == k, face[k], out)
        return out

    def unshare(plane, c):
        row, lane = iota(plane.shape, 0) % 2, iota(plane.shape, 1) % 2
        out = []
        for k in range(c):
            i, j = k // 2, k % 2
            w = jnp.where(lane == j, plane, roll(plane, 1 - 2 * j, 1))
            out.append(jnp.where(row == i, w, roll(w, 1 - 2 * i, 0)))
        return jnp.stack(out)[:, None]

    def send(r, v, s):
        xs, _, ys, _, zs, _ = bufs[r]
        c, nx = v.shape[:2]
        if s == 1:
            xs[0] = v[:, nx - 1]
            xs[1] = v[:, 0]
        else:
            xs[0, 0] = share(v[:, nx - 1])
            xs[1, 0] = share(v[:, 0])
        ys[0] = v[:, :, ny - 1 : ny]
        ys[1] = v[:, :, 0:1]
        if s == 1:
            start(r, 0)
            start(r, 1)
        place = ((iota((ny, nz), 1) + s) % nz) // (2 * s)
        packed = jnp.zeros((ny, nz), jnp.float32)
        for p in range(c * nx):
            packed = jnp.where(place == p, roll(v[p // nx, p % nx], 2 * s * p, 1), packed)
        zs[...] = packed
        start(r, 2)
        if s > 1:
            start(r, 0)
            start(r, 1)

    def z_halo(r, s, c, nx):
        zr = bufs[r][5]
        even = (iota((ny, nz), 1) & s) == 0
        w = jnp.where(even, roll(zr[0], s, 1), roll(zr[1], -s, 1))
        planes = [roll(w, -2 * s * p, 1) for p in range(c * nx)]
        return jnp.stack(planes).reshape(c, nx, ny, nz)

    def set_coef(level, lows, ups):
        ref = coef[level]
        s = 2**level
        row, lane = iota((1, ny, nz), 1), iota((1, ny, nz), 2)
        zero = 0.0
        ref[0] = lows[0]
        ref[1] = ups[0]
        ref[2] = jnp.where(row >= s, lows[1], zero)
        ref[3] = jnp.where(row < ny - s, ups[1], zero)
        ref[4] = jnp.where(lane >= s, lows[2], zero)
        ref[5] = jnp.where(lane < nz - s, ups[2], zero)
        ref[6] = jnp.where(row < s, lows[1], jnp.where(row >= ny - s, ups[1], zero))
        ref[7] = jnp.where(lane < s, lows[2], jnp.where(lane >= nz - s, ups[2], zero))

    def local_sum(level, v):
        ref = coef[level]
        s = 2**level
        edge = jnp.zeros_like(v[:, :1])
        total = ref[0] * jnp.concatenate([edge, v[:, :-1]], 1)
        total = total + ref[1] * jnp.concatenate([v[:, 1:], edge], 1)
        total = total + ref[2] * roll(v, s, 2) + ref[3] * roll(v, -s, 2)
        return total + ref[4] * roll(v, s, 3) + ref[5] * roll(v, -s, 3)

    def halo_sum(level, r, total):
        ref = coef[level]
        s = 2**level
        _, xr, _, yr, _, _ = bufs[r]
        nx = total.shape[1]
        sent_all(r - 1)
        for a in range(3):
            wait(r, a)
        faces = [xr[i][:, None] if s == 1 else unshare(xr[i, 0], total.shape[0]) for i in (0, 1)]
        first = total[:, :1] + ref[0, 0:1] * faces[0]
        last = total[:, nx - 1 :] + ref[1, nx - 1 : nx] * faces[1]
        middle = [total[:, 1 : nx - 1]] if nx > 2 else []
        total = jnp.concatenate([first] + middle + [last], 1)
        top = total[:, :, :half] + ref[6, :, :half] * yr[0]
        bottom = total[:, :, half:] + ref[6, :, half:] * yr[1]
        total = jnp.concatenate([top, bottom], 2)
        return total + ref[7] * z_halo(r, s, total.shape[0], nx)

    def neighbours(level, r, v):
        send(r, v, 2**level)
        return halo_sum(level, r, local_sum(level, v))

    def coarse_links(level, lows, ups):
        s = 2**level
        nx = lows[0].shape[0]
        row = iota((1, ny, nz), 1) & s
        lane = iota((1, ny, nz), 2) & s

        def along_x(links, offset):
            w = links.reshape(nx // 2, 2, ny, nz)[:, offset]
            return pair_sum(pair_sum(w, s, 1), s, 2)

        low = [
            along_x(lows[0], 0),
            restrict(jnp.where(row == 0, lows[1], 0.0), s),
            restrict(jnp.where(lane == 0, lows[2], 0.0), s),
        ]
        up = [
            along_x(ups[0], 1),
            restrict(jnp.where(row != 0, ups[1], 0.0), s),
            restrict(jnp.where(lane != 0, ups[2], 0.0), s),
        ]
        return low, up

    def diagonal(lows, ups, spring):
        return lows[0] + lows[1] + lows[2] + ups[0] + ups[1] + ups[2] + spring

    loads[0].wait()
    fraction = (den[...].astype(jnp.float32) + 1.0) / BINS
    modulus = 0.05 + 0.95 * fraction * fraction * fraction
    pl.semaphore_wait(barrier, greeted)
    send(0, modulus[None], 1)
    _, xr, _, yr, _, _ = bufs[0]
    row, lane = iota((1, ny, nz), 1), iota((1, ny, nz), 2)

    def shared(other):
        return jnp.where(other > 0.0, 0.5 * (modulus + other), 0.0)

    for a in range(3):
        wait(0, a)
    lows = [shared(jnp.concatenate([xr[0], modulus[:-1]], 0))]
    ups = [shared(jnp.concatenate([modulus[1:], xr[1]], 0))]
    lows.append(shared(jnp.where(row == 0, yr[0, 0], roll(modulus, 1, 1))))
    ups.append(shared(jnp.where(row == ny - 1, yr[1, 0], roll(modulus, -1, 1))))
    beside = z_halo(0, 1, 1, modulus.shape[0])[0]
    lows.append(shared(jnp.where(lane == 0, beside, roll(modulus, 1, 2))))
    ups.append(shared(jnp.where(lane == nz - 1, beside, roll(modulus, -1, 2))))
    spring = 0.1 * modulus

    loads[1].wait()
    loads[2].wait()
    fixed = fix[...].astype(jnp.float32)
    free_ref[...] = 1.0 - fixed
    diag_ref[...] = free_ref[...] * diagonal(lows, ups, spring) + fixed
    inv_ref[...] = 1.0 / diag_ref[...]
    fc0_ref[...] = damping * res[...] * inv_ref[...]

    masked = free_ref[...] * fc0_ref[...]
    send(1, masked, 1)
    set_coef(0, lows, ups)
    total = local_sum(0, masked)
    lows, ups = coarse_links(0, lows, ups)
    spring = restrict(spring, 1)
    inv1_ref[...] = 1.0 / diagonal(lows, ups, spring)
    total = halo_sum(0, 1, total)
    mid_rhs = restrict((1.0 - damping) * res[...] + free_ref[...] * total, 1)
    mid0 = damping * mid_rhs * inv1_ref[...]
    send(2, mid0, 2)
    set_coef(1, lows, ups)
    total = local_sum(1, mid0)
    lows, ups = coarse_links(1, lows, ups)
    spring = restrict(spring, 2)
    set_coef(2, lows, ups)
    inv2_ref[...] = 1.0 / diagonal(lows, ups, spring)
    total = halo_sum(1, 2, total)
    scaled_rhs = restrict((1.0 - damping) * mid_rhs + total, 2) * inv2_ref[...]

    ratio = eig_center / eig_halfwidth
    factor = 1.0 / ratio
    update = scaled_rhs / eig_center
    iterate = update
    for step in range(SWEEPS - 1):
        remainder = scaled_rhs - iterate + neighbours(2, 3 + step, iterate) * inv2_ref[...]
        next_factor = 1.0 / (2.0 * ratio - factor)
        update = next_factor * factor * update + 2.0 * next_factor / eig_halfwidth * remainder
        iterate = iterate + update
        factor = next_factor

    mid = mid0 + prolong(iterate)
    mid = (1.0 - damping) * mid + mid0 + damping * neighbours(1, 5, mid) * inv1_ref[...]
    fine = fc0_ref[...] + prolong(mid)
    total = neighbours(0, 6, free_ref[...] * fine)
    base = (1.0 - damping) * fine + fc0_ref[...]
    change = damping * free_ref[...] * total * inv_ref[...]
    out_b[...] = base
    out_c[...] = change
    direction = base + change
    masked = free_ref[...] * direction
    send(7, masked, 1)

    def fold(v):
        w = jnp.sum(jnp.sum(v.reshape(-1, 8, nz), axis=0), axis=0, keepdims=True)
        return w + roll(w, nz // 2, 1)

    precond = fold(res[...] * direction)
    image = diag_ref[...] * direction
    curve = fold(direction * image)
    out_r[...] = image
    total = halo_sum(0, 7, local_sum(0, masked)) * free_ref[...]
    curve = curve - fold((out_b[...] + out_c[...]) * total)
    out_r[...] = out_r[...] - total
    head = iota((1, nz), 1) < nz // 2
    mine = jnp.where(head, precond, curve)

    sent_all(n_rounds - 1)

    for g, group in enumerate(groups):
        buf = sums[g]
        size = group_size(counts, group)
        own = 0
        for a in group:
            own = own * counts[a] + idx[a]
        part[g] = mine
        buf[own] = mine

        def hop(k, slot):
            return pltpu.make_async_remote_copy(
                src_ref=part.at[g],
                dst_ref=buf.at[slot],
                send_sem=ssend_sem.at[g, k],
                recv_sem=srecv_sem.at[g, k],
                device_id=partner(group, k)[0],
                device_id_type=pl.DeviceIdType.MESH,
            )

        hops = [hop(k, own) for k in range(1, size)]
        for h in hops:
            h.start()
        for h in hops:
            h.wait_send()
        for k in range(1, size):
            hop(k, partner(group, -k)[1]).wait_recv()
        mine = jnp.sum(buf[...], axis=0)

    def grand(keep):
        return jnp.sum(jnp.where(keep, mine, 0.0), axis=1, keepdims=True)

    alpha = grand(head) / grand(jnp.logical_not(head))
    out_a[...] = jnp.broadcast_to(alpha, out_a.shape)


def shards(counts, solution, residual, density_bins, fixed_dofs):
    comps, nx, ny, nz = residual.shape
    f32 = jnp.float32
    scratch = []
    for level in ROUNDS:
        c, planes = (1, nx) if level == "bins" else (comps, nx // 2**level)
        face = 1 if level in (1, 2) else c
        scratch += [
            pltpu.VMEM((2, face, ny, nz), f32),
            pltpu.VMEM((2, face, ny, nz), f32),
            pltpu.VMEM((2, c, planes, 1, nz), f32),
            pltpu.VMEM((2, c, planes, 1, nz), f32),
            pltpu.VMEM((ny, nz), f32),
            pltpu.VMEM((2, ny, nz), f32),
        ]
    scratch += [pltpu.VMEM((8, nx // 2**level, ny, nz), f32) for level in range(3)]
    scratch += [pltpu.VMEM((comps, nx, ny, nz), f32)] * 4
    scratch += [pltpu.VMEM((nx // 2, ny, nz), f32), pltpu.VMEM((nx // 4, ny, nz), f32)]
    sizes = [group_size(counts, g) for g in sum_groups(counts)]
    scratch += [
        pltpu.VMEM((len(sizes), 1, nz), f32),
        pltpu.SemaphoreType.DMA((len(ROUNDS), 6)),
        pltpu.SemaphoreType.DMA((len(ROUNDS), 6)),
        pltpu.SemaphoreType.DMA((len(sizes), max(sizes))),
        pltpu.SemaphoreType.DMA((len(sizes), max(sizes))),
    ]
    scratch += [pltpu.VMEM((size, 1, nz), f32) for size in sizes]
    scratch += [
        pltpu.VMEM(residual.shape, f32),
        pltpu.VMEM(density_bins.shape, jnp.int32),
        pltpu.VMEM(fixed_dofs.shape, jnp.int32),
        pltpu.SemaphoreType.DMA((3,)),
    ]
    operands = [
        pltpu.with_memory_space_constraint(x, pltpu.HBM)
        for x in (residual, density_bins, fixed_dofs)
    ]
    shape = jax.ShapeDtypeStruct(residual.shape, f32)
    image, base, change, alpha = pl.pallas_call(
        functools.partial(kernel, counts),
        out_shape=(shape, shape, shape, jax.ShapeDtypeStruct((1, nz), f32)),
        in_specs=[pl.BlockSpec(memory_space=pltpu.HBM)] * 3,
        out_specs=(pl.BlockSpec(memory_space=pltpu.VMEM),) * 4,
        scratch_shapes=scratch,
        compiler_params=pltpu.CompilerParams(
            collective_id=0, has_side_effects=True, vmem_limit_bytes=32 * 2**20
        ),
    )(*operands)
    direction = base + change
    return (solution + alpha * direction, residual - alpha * image, direction)


def solution(mesh):
    counts = tuple(mesh.shape[a] for a in AXES)
    return jax.shard_map(
        functools.partial(shards, counts),
        mesh=mesh,
        in_specs=(P(None, *AXES), P(None, *AXES), P(*AXES), P(None, *AXES)),
        out_specs=(P(None, *AXES), P(None, *AXES), P(None, *AXES)),
        check_vma=False,
    )
```

```python
import functools

import jax
import jax.numpy as jnp
from jax import lax
from jax.experimental import pallas as pl
from jax.experimental.pallas import tpu as pltpu
from jax.sharding import PartitionSpec as P

SWEEPS = 3
BINS = 16
AXES = ("gx", "gy", "gz")

damping = 0.6
eig_center = 1.05
eig_halfwidth = 0.95

ROUNDS = ("bins", 0, 1, 2, 2, 1, 0, 0)


def roll(v, shift, axis):
    shift = shift % v.shape[axis]
    return v if shift == 0 else pltpu.roll(v, shift, axis)


def iota(shape, dim):
    return lax.broadcasted_iota(jnp.int32, shape, dim)


def pair_sum(v, s, axis):
    shape = (1,) * (v.ndim - 2) + v.shape[-2:]
    even = jnp.broadcast_to((iota(shape, axis) & s) == 0, v.shape)
    return v + jnp.where(even, roll(v, -s, axis), roll(v, s, axis))


def restrict(v, s):
    lead = v.shape[:-3]
    nx, ny, nz = v.shape[-3:]
    w = v.reshape(lead + (nx // 2, 2, ny, nz))
    k = len(lead) + 1
    w = lax.index_in_dim(w, 0, k, False) + lax.index_in_dim(w, 1, k, False)
    return pair_sum(pair_sum(w, s, w.ndim - 2), s, w.ndim - 1)


def prolong(v):
    c, nx, ny, nz = v.shape
    return jnp.broadcast_to(v[:, :, None], (c, nx, 2, ny, nz)).reshape(c, 2 * nx, ny, nz)


def sum_groups(counts):
    total = counts[0] * counts[1] * counts[2]
    return ((1, 2), (0,)) if total <= 64 else ((2,), (1,), (0,))


def group_size(counts, group):
    size = 1
    for a in group:
        size *= counts[a]
    return size


def kernel(counts, res_hbm, den_hbm, fix_hbm, out_r, out_b, out_c, out_a, *scratch):
    n_rounds = len(ROUNDS)
    res, den, fix, load_sem = scratch[-4:]
    loads = [
        pltpu.make_async_copy(src, dst, load_sem.at[i])
        for i, (src, dst) in enumerate(
            ((den_hbm, den), (res_hbm, res), (fix_hbm, fix))
        )
    ]
    for load in loads:
        load.start()
    bufs = [scratch[6 * r : 6 * r + 6] for r in range(n_rounds)]
    rest = scratch[6 * n_rounds :]
    coef = rest[0:3]
    free_ref, diag_ref, inv_ref, fc0_ref, inv1_ref, inv2_ref = rest[3:9]
    part, send_sem, recv_sem, ssend_sem, srecv_sem = rest[9:14]
    sums = rest[14:-4]
    groups = sum_groups(counts)

    idx = [lax.axis_index(a) for a in AXES]
    ny, nz = den.shape[1:]
    half = ny // 2

    barrier = pltpu.get_barrier_semaphore()


    def partner(group, k):
        there, place, left = {}, 0, abs(k)
        for a in reversed(group):
            step = left % counts[a]
            left //= counts[a]
            there[a] = lax.rem(idx[a] + (step if k > 0 else counts[a] - step), counts[a])
        for a in group:
            place = place * counts[a] + there[a]
        return {AXES[a]: there[a] for a in group}, place

    greeted = 0
    for group in groups:
        for k in range(1, group_size(counts, group)):
            pl.semaphore_signal(
                barrier,
                inc=1,
                device_id=partner(group, k)[0],
                device_id_type=pl.DeviceIdType.MESH,
            )
            greeted += 1

    for a in range(3):
        for side, beyond in enumerate((idx[a] == 0, idx[a] == counts[a] - 1)):

            @pl.when(beyond)
            def _():
                for r in range(n_rounds):
                    ref = bufs[r][2 * a + 1]
                    ref[side] = jnp.zeros(ref.shape[1:], jnp.float32)

    def copies(r, a):
        xs, xr, ys, yr, zs, zr = bufs[r]
        for up in (0, 1):
            if a == 0:
                src, dst = xs.at[up], xr.at[up]
            elif a == 1:
                src, dst = ys.at[up], yr.at[up]
            else:
                src, dst = zs, zr.at[up]
            slot = 2 * a + up
            yield pltpu.make_async_remote_copy(
                src_ref=src,
                dst_ref=dst,
                send_sem=send_sem.at[r, slot],
                recv_sem=recv_sem.at[r, slot],
                device_id={AXES[a]: idx[a] - 1 if up else idx[a] + 1},
                device_id_type=pl.DeviceIdType.MESH,
            )

    def has_next(a):
        return idx[a] < counts[a] - 1

    def has_prev(a):
        return idx[a] > 0

    def start(r, a):
        to_next, to_prev = copies(r, a)
        pl.when(has_next(a))(to_next.start)
        pl.when(has_prev(a))(to_prev.start)

    def wait(r, a):
        to_next, to_prev = copies(r, a)
        pl.when(has_prev(a))(to_next.wait_recv)
        pl.when(has_next(a))(to_prev.wait_recv)

    def sent_all(r):
        for a in range(3):
            to_next, to_prev = copies(r, a)
            pl.when(has_next(a))(to_next.wait_send)
            pl.when(has_prev(a))(to_prev.wait_send)

    def share(face):
        slot = 2 * (iota(face.shape[1:], 0) % 2) + iota(face.shape[1:], 1) % 2
        out = face[0]
        for k in range(1, face.shape[0]):
            out = jnp.where(slot == k, face[k], out)
        return out

    def unshare(plane, c):
        row, lane = iota(plane.shape, 0) % 2, iota(plane.shape, 1) % 2
        out = []
        for k in range(c):
            i, j = k // 2, k % 2
            w = jnp.where(lane == j, plane, roll(plane, 1 - 2 * j, 1))
            out.append(jnp.where(row == i, w, roll(w, 1 - 2 * i, 0)))
        return jnp.stack(out)[:, None]

    def send(r, v, s):
        xs, _, ys, _, zs, _ = bufs[r]
        c, nx = v.shape[:2]
        if s == 1:
            xs[0] = v[:, nx - 1]
            xs[1] = v[:, 0]
        else:
            xs[0, 0] = share(v[:, nx - 1])
            xs[1, 0] = share(v[:, 0])
        ys[0] = v[:, :, ny - 1 : ny]
        ys[1] = v[:, :, 0:1]
        if s == 1:
            start(r, 0)
            start(r, 1)
        place = ((iota((ny, nz), 1) + s) % nz) // (2 * s)
        packed = jnp.zeros((ny, nz), jnp.float32)
        for p in range(c * nx):
            packed = jnp.where(place == p, roll(v[p // nx, p % nx], 2 * s * p, 1), packed)
        zs[...] = packed
        start(r, 2)
        if s > 1:
            start(r, 0)
            start(r, 1)

    def z_halo(r, s, c, nx):
        zr = bufs[r][5]
        even = (iota((ny, nz), 1) & s) == 0
        w = jnp.where(even, roll(zr[0], s, 1), roll(zr[1], -s, 1))
        planes = [roll(w, -2 * s * p, 1) for p in range(c * nx)]
        return jnp.stack(planes).reshape(c, nx, ny, nz)

    def set_coef(level, lows, ups):
        ref = coef[level]
        s = 2**level
        row, lane = iota((1, ny, nz), 1), iota((1, ny, nz), 2)
        zero = 0.0
        ref[0] = lows[0]
        ref[1] = ups[0]
        ref[2] = jnp.where(row >= s, lows[1], zero)
        ref[3] = jnp.where(row < ny - s, ups[1], zero)
        ref[4] = jnp.where(lane >= s, lows[2], zero)
        ref[5] = jnp.where(lane < nz - s, ups[2], zero)
        ref[6] = jnp.where(row < s, lows[1], jnp.where(row >= ny - s, ups[1], zero))
        ref[7] = jnp.where(lane < s, lows[2], jnp.where(lane >= nz - s, ups[2], zero))

    def local_sum(level, v):
        ref = coef[level]
        s = 2**level
        edge = jnp.zeros_like(v[:, :1])
        total = ref[0] * jnp.concatenate([edge, v[:, :-1]], 1)
        total = total + ref[1] * jnp.concatenate([v[:, 1:], edge], 1)
        total = total + ref[2] * roll(v, s, 2) + ref[3] * roll(v, -s, 2)
        return total + ref[4] * roll(v, s, 3) + ref[5] * roll(v, -s, 3)

    def halo_sum(level, r, total):
        ref = coef[level]
        s = 2**level
        _, xr, _, yr, _, _ = bufs[r]
        nx = total.shape[1]
        sent_all(r - 1)
        for a in range(3):
            wait(r, a)
        faces = [xr[i][:, None] if s == 1 else unshare(xr[i, 0], total.shape[0]) for i in (0, 1)]
        first = total[:, :1] + ref[0, 0:1] * faces[0]
        last = total[:, nx - 1 :] + ref[1, nx - 1 : nx] * faces[1]
        middle = [total[:, 1 : nx - 1]] if nx > 2 else []
        total = jnp.concatenate([first] + middle + [last], 1)
        top = total[:, :, :half] + ref[6, :, :half] * yr[0]
        bottom = total[:, :, half:] + ref[6, :, half:] * yr[1]
        total = jnp.concatenate([top, bottom], 2)
        return total + ref[7] * z_halo(r, s, total.shape[0], nx)

    def neighbours(level, r, v):
        send(r, v, 2**level)
        return halo_sum(level, r, local_sum(level, v))

    def coarse_links(level, lows, ups):
        s = 2**level
        nx = lows[0].shape[0]
        row = iota((1, ny, nz), 1) & s
        lane = iota((1, ny, nz), 2) & s

        def along_x(links, offset):
            w = links.reshape(nx // 2, 2, ny, nz)[:, offset]
            return pair_sum(pair_sum(w, s, 1), s, 2)

        low = [
            along_x(lows[0], 0),
            restrict(jnp.where(row == 0, lows[1], 0.0), s),
            restrict(jnp.where(lane == 0, lows[2], 0.0), s),
        ]
        up = [
            along_x(ups[0], 1),
            restrict(jnp.where(row != 0, ups[1], 0.0), s),
            restrict(jnp.where(lane != 0, ups[2], 0.0), s),
        ]
        return low, up

    def diagonal(lows, ups, spring):
        return lows[0] + lows[1] + lows[2] + ups[0] + ups[1] + ups[2] + spring

    loads[0].wait()
    fraction = (den[...].astype(jnp.float32) + 1.0) / BINS
    modulus = 0.05 + 0.95 * fraction * fraction * fraction
    pl.semaphore_wait(barrier, greeted)
    send(0, modulus[None], 1)
    _, xr, _, yr, _, _ = bufs[0]
    row, lane = iota((1, ny, nz), 1), iota((1, ny, nz), 2)

    def shared(other):
        return jnp.where(other > 0.0, 0.5 * (modulus + other), 0.0)

    for a in range(3):
        wait(0, a)
    lows = [shared(jnp.concatenate([xr[0], modulus[:-1]], 0))]
    ups = [shared(jnp.concatenate([modulus[1:], xr[1]], 0))]
    lows.append(shared(jnp.where(row == 0, yr[0, 0], roll(modulus, 1, 1))))
    ups.append(shared(jnp.where(row == ny - 1, yr[1, 0], roll(modulus, -1, 1))))
    beside = z_halo(0, 1, 1, modulus.shape[0])[0]
    lows.append(shared(jnp.where(lane == 0, beside, roll(modulus, 1, 2))))
    ups.append(shared(jnp.where(lane == nz - 1, beside, roll(modulus, -1, 2))))
    spring = 0.1 * modulus

    loads[1].wait()
    loads[2].wait()
    fixed = fix[...].astype(jnp.float32)
    free_ref[...] = 1.0 - fixed
    diag_ref[...] = free_ref[...] * diagonal(lows, ups, spring) + fixed
    inv_ref[...] = 1.0 / diag_ref[...]
    fc0_ref[...] = damping * res[...] * inv_ref[...]

    masked = free_ref[...] * fc0_ref[...]
    send(1, masked, 1)
    set_coef(0, lows, ups)
    total = local_sum(0, masked)
    lows, ups = coarse_links(0, lows, ups)
    spring = restrict(spring, 1)
    inv1_ref[...] = 1.0 / diagonal(lows, ups, spring)
    total = halo_sum(0, 1, total)
    mid_rhs = restrict((1.0 - damping) * res[...] + free_ref[...] * total, 1)
    mid0 = damping * mid_rhs * inv1_ref[...]
    send(2, mid0, 2)
    set_coef(1, lows, ups)
    total = local_sum(1, mid0)
    lows, ups = coarse_links(1, lows, ups)
    spring = restrict(spring, 2)
    set_coef(2, lows, ups)
    inv2_ref[...] = 1.0 / diagonal(lows, ups, spring)
    total = halo_sum(1, 2, total)
    scaled_rhs = restrict((1.0 - damping) * mid_rhs + total, 2) * inv2_ref[...]

    ratio = eig_center / eig_halfwidth
    factor = 1.0 / ratio
    update = scaled_rhs / eig_center
    iterate = update
    for step in range(SWEEPS - 1):
        remainder = scaled_rhs - iterate + neighbours(2, 3 + step, iterate) * inv2_ref[...]
        next_factor = 1.0 / (2.0 * ratio - factor)
        update = next_factor * factor * update + 2.0 * next_factor / eig_halfwidth * remainder
        iterate = iterate + update
        factor = next_factor

    mid = mid0 + prolong(iterate)
    mid = (1.0 - damping) * mid + mid0 + damping * neighbours(1, 5, mid) * inv1_ref[...]
    fine = fc0_ref[...] + prolong(mid)
    total = neighbours(0, 6, free_ref[...] * fine)
    base = (1.0 - damping) * fine + fc0_ref[...]
    change = damping * free_ref[...] * total * inv_ref[...]
    out_b[...] = base
    out_c[...] = change
    direction = base + change
    masked = free_ref[...] * direction
    send(7, masked, 1)

    def fold(v):
        w = jnp.sum(jnp.sum(v.reshape(-1, 8, nz), axis=0), axis=0, keepdims=True)
        return w + roll(w, nz // 2, 1)

    precond = fold(res[...] * direction)
    image = diag_ref[...] * direction
    curve = fold(direction * image)
    out_r[...] = image
    total = halo_sum(0, 7, local_sum(0, masked)) * free_ref[...]
    curve = curve - fold((out_b[...] + out_c[...]) * total)
    out_r[...] = out_r[...] - total
    head = iota((1, nz), 1) < nz // 2
    mine = jnp.where(head, precond, curve)

    sent_all(n_rounds - 1)

    for g, group in enumerate(groups):
        buf = sums[g]
        size = group_size(counts, group)
        own = 0
        for a in group:
            own = own * counts[a] + idx[a]
        part[g] = mine
        buf[own] = mine

        def hop(k, slot):
            return pltpu.make_async_remote_copy(
                src_ref=part.at[g],
                dst_ref=buf.at[slot],
                send_sem=ssend_sem.at[g, k],
                recv_sem=srecv_sem.at[g, k],
                device_id=partner(group, k)[0],
                device_id_type=pl.DeviceIdType.MESH,
            )

        hops = [hop(k, own) for k in range(1, size)]
        for h in hops:
            h.start()
        for h in hops:
            h.wait_send()
        for k in range(1, size):
            hop(k, partner(group, -k)[1]).wait_recv()
        mine = jnp.sum(buf[...], axis=0)

    def grand(keep):
        return jnp.sum(jnp.where(keep, mine, 0.0), axis=1, keepdims=True)

    alpha = grand(head) / grand(jnp.logical_not(head))
    out_a[...] = jnp.broadcast_to(alpha, out_a.shape)


def shards(counts, solution, residual, density_bins, fixed_dofs):
    comps, nx, ny, nz = residual.shape
    f32 = jnp.float32
    scratch = []
    for level in ROUNDS:
        c, planes = (1, nx) if level == "bins" else (comps, nx // 2**level)
        face = 1 if level in (1, 2) else c
        scratch += [
            pltpu.VMEM((2, face, ny, nz), f32),
            pltpu.VMEM((2, face, ny, nz), f32),
            pltpu.VMEM((2, c, planes, 1, nz), f32),
            pltpu.VMEM((2, c, planes, 1, nz), f32),
            pltpu.VMEM((ny, nz), f32),
            pltpu.VMEM((2, ny, nz), f32),
        ]
    scratch += [pltpu.VMEM((8, nx // 2**level, ny, nz), f32) for level in range(3)]
    scratch += [pltpu.VMEM((comps, nx, ny, nz), f32)] * 4
    scratch += [pltpu.VMEM((nx // 2, ny, nz), f32), pltpu.VMEM((nx // 4, ny, nz), f32)]
    sizes = [group_size(counts, g) for g in sum_groups(counts)]
    scratch += [
        pltpu.VMEM((len(sizes), 1, nz), f32),
        pltpu.SemaphoreType.DMA((len(ROUNDS), 6)),
        pltpu.SemaphoreType.DMA((len(ROUNDS), 6)),
        pltpu.SemaphoreType.DMA((len(sizes), max(sizes))),
        pltpu.SemaphoreType.DMA((len(sizes), max(sizes))),
    ]
    scratch += [pltpu.VMEM((size, 1, nz), f32) for size in sizes]
    scratch += [
        pltpu.VMEM(residual.shape, f32),
        pltpu.VMEM(density_bins.shape, jnp.int32),
        pltpu.VMEM(fixed_dofs.shape, jnp.int32),
        pltpu.SemaphoreType.DMA((3,)),
    ]
    operands = [
        pltpu.with_memory_space_constraint(x, pltpu.HBM)
        for x in (residual, density_bins, fixed_dofs)
    ]
    shape = jax.ShapeDtypeStruct(residual.shape, f32)
    image, base, change, alpha = pl.pallas_call(
        functools.partial(kernel, counts),
        out_shape=(shape, shape, shape, jax.ShapeDtypeStruct((1, nz), f32)),
        in_specs=[pl.BlockSpec(memory_space=pltpu.HBM)] * 3,
        out_specs=(pl.BlockSpec(memory_space=pltpu.VMEM),) * 4,
        scratch_shapes=scratch,
        compiler_params=pltpu.CompilerParams(
            collective_id=0, has_side_effects=True, vmem_limit_bytes=32 * 2**20
        ),
    )(*operands)
    direction = base + change
    return (solution + alpha * direction, residual - alpha * image, direction)


def solution(mesh):
    counts = tuple(mesh.shape[a] for a in AXES)
    return jax.shard_map(
        functools.partial(shards, counts),
        mesh=mesh,
        in_specs=(P(None, *AXES), P(None, *AXES), P(*AXES), P(None, *AXES)),
        out_specs=(P(None, *AXES), P(None, *AXES), P(None, *AXES)),
        check_vma=False,
    )
```
